32 devices in a mesh: dp: 16 (over z, y, core), mp: 2 (over x).
Axes of the slice: x: 2, y: 2, z: 4, core: 2. Of those that a mesh axis runs over, the one named last changes fastest.
Arguments:
- attention: bfloat16 [2048, 2048], P('dp', 'mp'), may hold values from -6 to 6
- residual: bfloat16 [2048, 2048], P('dp', 'mp'), may hold values from -6 to 6
- out_weight: bfloat16 [2048, 2048], P('mp', 'dp'), may hold values from -0.125 to 0.125
- ffn_gain: float32 [2048], P('mp'), may hold values from 0.1 to 1.9
- shared_gate: bfloat16 [2048, 2816], P('dp', 'mp'), may hold values from -0.125 to 0.125
- shared_up: bfloat16 [2048, 2816], P('dp', 'mp'), may hold values from -0.125 to 0.125
- shared_down: bfloat16 [2816, 2048], P('mp', 'dp'), may hold values from -0.109375 to 0.109375
- expert_gate: bfloat16 [16, 2048, 1408], P('dp', None, 'mp'), may hold values from -0.125 to 0.125
- expert_up: bfloat16 [16, 2048, 1408], P('dp', None, 'mp'), may hold values from -0.125 to 0.125
- expert_down: bfloat16 [16, 1408, 2048], P('dp', 'mp'), may hold values from -0.15625 to 0.15625
- route_ids: int32 [2048, 6], P('dp'), may hold values from 0 to 15, all different within a row; in each aligned block of 128 rows (0 to 127, 128 to 255, ...) at most 64 rows name the same one
- route_scores: float32 [2048, 6], P('dp'), may hold values from 0.05 to 1
- placement: int32 [16], replicated, may hold values from 0 to 15, each once
- next_gain: float32 [2048], P('mp'), may hold values from 0.1 to 1.9
Outputs:
- final: bfloat16 [2048, 2048], P('dp', 'mp')
- next_normed: bfloat16 [2048, 2048], P('dp', 'mp')
The draws below stay inside these ranges and needn't reach their ends.
Inputs may be any that keep to these rules, and one draw needn't show every extreme that they name: `route_ids`: A token's 6 experts differ. In each aligned block of 128 rows (the rows of one index of dp) no expert is named by more than 64 rows, a bound that some block reaches. `placement`: each storage index is used by exactly one expert.
All inputs are finite; a program needn't handle non-finite values.
Results may differ from the reference program's by a relative error of at most 0.0075.
Values may be sent and summed in bfloat16 or wider, within the bound.
No kernel may reach another device: no remote copies, remote signals or barrier semaphores. Data moves between devices by JAX's collectives and lax.ppermute only.
A program may use at most 128 MiB of HBM per device.

```python
import math
import jax
import jax.numpy as jnp
import numpy as np
from jax import lax

D = 2048
FFE = 1408
TOP = 6
TOK_DEV = 128
EXPERTS = 16
SH = 2816
CAP = 64
TOKENS = 2048
N_DP = 16


def level_of(rng, shape, split, least, largest):
    level = 1.0
    for axis_at, shards_of in split:
        heights = jax.random.uniform(jax.random.fold_in(jax.random.fold_in(rng, 6), axis_at), (shards_of,), jnp.float32, least / len(split), largest / len(split))
        level = level * jnp.repeat(jnp.exp(heights), shape[axis_at] // shards_of).reshape((-1,) + (1,) * (len(shape) - 1 - axis_at))
    return level


def assign_block(rng, own, number, rows, number_of, top, limit, slope):
    order = jax.random.permutation(rng, number_of)
    heavy_load, usual = shares(number_of, rows * top, limit, slope, True), shares(number_of, rows * top, limit, slope, False)
    places = jnp.arange(number_of)

    def named(tallies, offset_by):
        used = int((tallies > 0).sum())
        fixed = max(1, used // 4)
        moved = fixed + (places - fixed + offset_by * (used - fixed)) % max(1, number_of - fixed)
        return jnp.zeros((number_of,), jnp.int32).at[order[jnp.where(places < fixed, places, moved)]].set(jnp.asarray(tallies, jnp.int32))

    tallies = jnp.where(number % 4 == 0, named(heavy_load, number // 4), named(usual, number - number // 4 - 1))
    mixed = jax.random.permutation(jax.random.fold_in(own, 3), number_of)
    giver, taker = mixed[0:number_of // 2 * 2:2], mixed[1:number_of // 2 * 2:2]
    margin = jnp.minimum(tallies[giver] - 1, limit - tallies[taker]) // 2
    margin = jnp.where((giver == order[0]) | (taker == order[0]) | (tallies[taker] == 0), 0, jnp.maximum(margin, 0))
    moved = jax.random.randint(jax.random.fold_in(own, 4), (number_of // 2,), 0, 1 << 20) % (margin + 1)
    tallies = tallies.at[giver].add(-moved).at[taker].add(moved)
    labels = jnp.searchsorted(jnp.cumsum(tallies), jnp.arange(rows * top), side="right").astype(jnp.int32)
    grid = labels.reshape(top, rows).T
    grid = grid[jax.random.permutation(jax.random.fold_in(own, 1), rows)]
    offset_by = jax.random.randint(jax.random.fold_in(own, 2), (rows, 1), 0, top)
    return jnp.take_along_axis(grid, (jnp.arange(top)[None, :] + offset_by) % top, axis=1)


def shares(number_of, total, most, skew, full):
    loads = [(1 << 20) // math.isqrt(rank ** skew) + 1 for rank in range(1, number_of + 1)]
    largest = most if full else min(most, max(-(-total // number_of), total * loads[0] // sum(loads)))
    least = 1 if total - largest >= number_of - 1 else 0
    counts, spare = [largest] + [least] * (number_of - 1), total - largest - least * (number_of - 1)
    while spare > 0:
        candidates = [i for i in range(1, number_of) if counts[i] < largest] or [i for i in range(1, number_of) if counts[i] < most]
        whole, remaining = sum([loads[i] for i in candidates]), spare
        for i in candidates:
            more = min(most - counts[i], max(1, remaining * loads[i] // whole), spare)
            counts[i] = counts[i] + more
            spare = spare - more
    return np.array(counts)


def normal_values(rng, shape, deviation, reach, shards=(), kind=jnp.bfloat16):
    array = jax.random.normal(rng, shape, jnp.float32) * deviation
    if len(shards) > 0:
        array = level_of(rng, shape, shards, -0.22, 0.18) * array
    return jnp.clip(array, min=-reach, max=reach).astype(kind)


def setup_inputs(seed: int = 0) -> dict:
    arg_keys = jax.random.split(jax.random.key(seed), 15)
    attention = normal_values(arg_keys[0], (TOKENS, D), 1.0, 6.0, ((0, 16), (1, 2)))
    residual = normal_values(arg_keys[1], (TOKENS, D), 1.0, 6.0, ((0, 16), (1, 2)))
    out_weight = normal_values(arg_keys[2], (D, D), D ** -0.5, 0.125, ((0, 2), (1, 16)))
    ffn_gain = jnp.clip(1.0 + 0.18 * jax.random.normal(arg_keys[3], (D,), jnp.float32), 0.1, 1.9)
    shared_gate = normal_values(arg_keys[4], (D, SH), D ** -0.5, 0.125, ((0, 16), (1, 2)))
    shared_up = normal_values(arg_keys[5], (D, SH), D ** -0.5, 0.125, ((0, 16), (1, 2)))
    shared_down = normal_values(arg_keys[6], (SH, D), SH ** -0.5, 0.109375, ((0, 2), (1, 16)))
    expert_gate = normal_values(arg_keys[7], (EXPERTS, D, FFE), D ** -0.5, 0.125, ((0, 16), (2, 2)))
    expert_up = normal_values(arg_keys[8], (EXPERTS, D, FFE), D ** -0.5, 0.125, ((0, 16), (2, 2)))
    expert_down = normal_values(arg_keys[9], (EXPERTS, FFE, D), FFE ** -0.5, 0.15625, ((0, 16), (1, 2)))
    route_ids_keys = jax.random.split(jax.random.fold_in(arg_keys[10], 1), TOKENS // TOK_DEV)
    route_ids_turns = jax.random.permutation(jax.random.fold_in(arg_keys[10], 3), TOKENS // TOK_DEV)
    route_ids = jax.vmap(lambda own, number: assign_block(jax.random.fold_in(arg_keys[10], 2), own, number, TOK_DEV, EXPERTS, TOP, CAP, 2))(route_ids_keys, route_ids_turns).reshape((TOKENS, TOP))
    route_scores = jnp.clip(jnp.exp(math.log(1.0) - 2.9957323 * jax.random.uniform(arg_keys[11], (TOKENS, TOP), jnp.float32) ** level_of(arg_keys[11], (TOKENS, TOP), ((0, 16),), -0.2, 0.2)), 0.05, 1.0)
    placement = jax.random.permutation(arg_keys[12], EXPERTS).astype(jnp.int32)
    next_gain = jnp.clip(1.0 + 0.18 * jax.random.normal(arg_keys[13], (D,), jnp.float32), 0.1, 1.9)
    return dict(attention=attention, residual=residual, out_weight=out_weight, ffn_gain=ffn_gain, shared_gate=shared_gate, shared_up=shared_up, shared_down=shared_down, expert_gate=expert_gate, expert_up=expert_up, expert_down=expert_down, route_ids=route_ids, route_scores=route_scores, placement=placement, next_gain=next_gain)


def rms_norm(values, gain):
    values = values.astype(jnp.float32)
    mean_sq = lax.optimization_barrier(jnp.mean(values * values, axis=1, keepdims=True))
    return (values * lax.rsqrt(mean_sq + 1e-06) * gain).astype(jnp.bfloat16)

def reference(attention, residual, out_weight, ffn_gain, shared_gate, shared_up, shared_down, expert_gate, expert_up, expert_down, route_ids, route_scores, placement, next_gain):
    projected = jnp.dot(attention, out_weight, preferred_element_type=jnp.float32)
    hidden = (residual.astype(jnp.float32) + projected).astype(jnp.bfloat16)
    normed = rms_norm(hidden, ffn_gain)
    shared_act = (jax.nn.silu(jnp.dot(normed, shared_gate, preferred_element_type=jnp.float32)) * jnp.dot(normed, shared_up, preferred_element_type=jnp.float32)).astype(jnp.bfloat16)
    shared_out = jnp.dot(shared_act, shared_down, preferred_element_type=jnp.float32)
    flat_ids = route_ids.reshape(N_DP, TOK_DEV * TOP)
    one_hot = (flat_ids[:, :, None] == jnp.arange(EXPERTS, dtype=jnp.int32)[None, None, :]).astype(jnp.int32)
    target = lax.optimization_barrier(jnp.sum(one_hot * placement[None, None, :], axis=2))
    slot = lax.optimization_barrier(jnp.sum((jnp.cumsum(one_hot, axis=1) - one_hot) * one_hot, axis=2))
    source = jnp.arange(N_DP, dtype=jnp.int32)[:, None]
    index = ((target * N_DP + source) * CAP + slot).reshape(-1)
    token = (source * TOK_DEV + jnp.arange(TOK_DEV * TOP, dtype=jnp.int32)[None, :] // TOP).reshape(-1)
    token_table = jnp.zeros((EXPERTS * N_DP * CAP,), jnp.int32).at[index].set(token.astype(jnp.int32))
    score_table = jnp.zeros((EXPERTS * N_DP * CAP,), route_scores.dtype).at[index].set(route_scores.reshape(-1))
    token_table = token_table.reshape(EXPERTS, N_DP * CAP)
    score_table = score_table.reshape(EXPERTS, N_DP * CAP)

    def one_expert(total, inputs):
        tokens_here, scores_here, gate_block, up_block, down_block = inputs
        in_rows = normed[tokens_here]
        activated = (jax.nn.silu(jnp.dot(in_rows, gate_block, preferred_element_type=jnp.float32)) * jnp.dot(in_rows, up_block, preferred_element_type=jnp.float32)).astype(jnp.bfloat16)
        out_rows = jnp.dot(activated, down_block, preferred_element_type=jnp.float32).astype(jnp.bfloat16)
        total = total.at[tokens_here].add(out_rows.astype(total.dtype) * scores_here[:, None])
        return (total, None)
    routed, _ = lax.scan(one_expert, jnp.zeros((N_DP * TOK_DEV, D), jnp.float32), (token_table, score_table, expert_gate, expert_up, expert_down))
    final = (hidden.astype(jnp.float32) + (shared_out + routed)).astype(jnp.bfloat16)
    return (final, rms_norm(final, next_gain))
```

```python
import jax
import jax.numpy as jnp
from jax import lax
from jax.sharding import PartitionSpec as P

D = 2048
EPSILON = 1e-06
CORES = 2
LANES = 128


def matmul(left, right):
    return jnp.dot(left, right, preferred_element_type=jnp.float32)


def chip_cycle(deep, wide):
    if deep == 1 or wide == 1:
        return list(range(deep * wide))
    walk = []
    for y in range(wide):
        line = range(1, deep) if y % 2 == 0 else range(deep - 1, 0, -1)
        walk += [z * wide + y for z in line]
    return walk + list(range(wide - 1, -1, -1))


class Moves:
    def __init__(self, dp_count, mp_count):
        self.chips = dp_count // CORES
        self.mp_count = mp_count
        wide = mp_count if self.chips % mp_count == 0 else 1
        self.cycle = chip_cycle(self.chips // wide, wide)
        self.place = [0] * self.chips
        for at, chip in enumerate(self.cycle):
            self.place[chip] = at
        self.left = self.chips // 2
        self.right = (self.chips - 1) // 2
        self.chip = lax.axis_index("dp") // CORES
        self.core = lax.axis_index("dp") % CORES
        self.mp = lax.axis_index("mp")
        self.at = jnp.asarray(self.place, jnp.int32)[self.chip]

    def step(self, value, way):
        count = self.chips
        pairs = [
            (self.cycle[i] * CORES + c, self.cycle[(i + way) % count] * CORES + c)
            for i in range(count)
            for c in range(CORES)
        ]
        return lax.ppermute(value, "dp", pairs)

    def swap_core(self, value):
        count = self.chips * CORES
        return lax.ppermute(value, "dp", [(d, d ^ 1) for d in range(count)])

    def from_mp(self, value, k):
        count = self.mp_count
        return lax.ppermute(value, "mp", [((i + k) % count, i) for i in range(count)])

    def chip_at(self, offset):
        return jnp.asarray(self.cycle, jnp.int32)[(self.at + offset) % self.chips]

    def gather_mp(self, value):
        whole = jnp.zeros((self.mp_count,) + value.shape, value.dtype)
        whole = lax.dynamic_update_index_in_dim(whole, value, self.mp, 0)
        for k in range(1, self.mp_count):
            whole = lax.dynamic_update_index_in_dim(
                whole, self.from_mp(value, k), (self.mp + k) % self.mp_count, 0
            )
        return whole

    def sum_mp(self, value):
        sent = value.astype(jnp.bfloat16)
        total = sent.astype(jnp.float32)
        for k in range(1, self.mp_count):
            total = total + self.from_mp(sent, k).astype(jnp.float32)
        return total

    def scatter_mp(self, value):
        total = lax.dynamic_index_in_dim(value, self.mp, 1, False)
        for k in range(1, self.mp_count):
            to = (self.mp - k) % self.mp_count
            part = lax.dynamic_index_in_dim(value, to, 1, False).astype(jnp.bfloat16)
            total = total + self.from_mp(part, k).astype(jnp.float32)
        return total


def local(
    attention,
    residual,
    out_weight,
    ffn_gain,
    shared_gate,
    shared_up,
    shared_down,
    expert_gate,
    expert_up,
    expert_down,
    route_ids,
    route_scores,
    placement,
    next_gain,
):
    rows, half = attention.shape
    mp_count = lax.axis_size("mp")
    dp_count = lax.axis_size("dp")
    moves = Moves(dp_count, mp_count)
    bf16, f32 = jnp.bfloat16, jnp.float32

    targets = placement[route_ids]
    storage = jnp.arange(dp_count, dtype=jnp.int32)
    own_scores = jnp.sum(
        jnp.where(targets[None] == storage[:, None, None], route_scores[None], 0.0), axis=2
    )
    scores = lax.all_to_all(own_scores, "dp", 0, 0, tiled=True)

    units = shared_gate.shape[1] // dp_count
    wide = shared_gate.shape[0]
    parts = [
        shared_gate.T.reshape(dp_count, units, wide),
        shared_up.T.reshape(dp_count, units, wide),
        shared_down.reshape(dp_count, units, wide),
    ]
    dealt = lax.all_to_all(jnp.concatenate(parts, axis=1), "dp", 0, 0, tiled=True)
    dealt = dealt.reshape(dp_count, 3, units, wide)
    hidden_units = expert_gate.shape[2]
    padded = -(-(hidden_units + units) // LANES) * LANES
    spare = padded - hidden_units - units
    columns = [dealt[:, i].transpose(0, 2, 1).reshape(D, units) for i in range(2)]
    gate_up = jnp.concatenate(
        [
            expert_gate[0],
            columns[0],
            jnp.zeros((D, spare), bf16),
            expert_up[0],
            columns[1],
            jnp.zeros((D, spare), bf16),
        ],
        axis=1,
    )
    down = jnp.concatenate(
        [
            expert_down[0],
            dealt[:, 2].transpose(1, 0, 2).reshape(units, D),
            jnp.zeros((spare, D), bf16),
        ],
        axis=0,
    )
    is_routed = jnp.arange(padded) < hidden_units

    whole_residual = moves.gather_mp(residual).transpose(1, 0, 2).reshape(rows, D)
    gain = moves.gather_mp(ffn_gain).reshape(D)
    both = jnp.concatenate([attention, moves.swap_core(attention)], axis=0)
    sums = jnp.zeros((moves.chips, CORES * rows, out_weight.shape[1]), f32)

    def project(sums, blocks):
        values = jnp.stack([matmul(both, w) for _, w in blocks])
        values = moves.sum_mp(values)
        for i, (offset, _) in enumerate(blocks):
            sums = lax.dynamic_update_index_in_dim(sums, values[i], moves.chip_at(offset), 0)
        return sums

    sums = project(sums, [(0, out_weight)])
    ahead = behind = out_weight
    for s in range(1, moves.left + 1):
        ahead = moves.step(ahead, 1)
        blocks = [(-s, ahead)]
        if s <= moves.right:
            behind = moves.step(behind, -1)
            blocks.append((s, behind))
        sums = project(sums, blocks)
    mine = sums[:, :rows]
    other = moves.swap_core(sums[:, rows:])
    first = jnp.where(moves.core == 0, mine, other)
    second = jnp.where(moves.core == 0, other, mine)
    projected = jnp.stack([first, second], axis=1).transpose(2, 0, 1, 3).reshape(rows, D)
    hidden = (whole_residual.astype(f32) + projected).astype(bf16)
    hidden_float = hidden.astype(f32)
    squares = jnp.sum(hidden_float * hidden_float, axis=1, keepdims=True)
    normed = (hidden_float * lax.rsqrt(squares / D + EPSILON) * gain).astype(bf16)

    def experts(offset, tokens):
        chip = moves.chip_at(offset)
        token_scores = [
            lax.dynamic_index_in_dim(scores, chip * CORES + c, 0, False)
            for c in (moves.core, 1 - moves.core)
        ]
        score = jnp.concatenate(token_scores)[:, None]
        values = matmul(jnp.concatenate([tokens, moves.swap_core(tokens)]), gate_up)
        scale = jnp.where(is_routed[None, :], score, 1.0)
        act = (jax.nn.silu(values[:, :padded]) * values[:, padded:] * scale).astype(bf16)
        out = matmul(act, down).astype(bf16)
        total = out[:rows].astype(f32) + moves.swap_core(out[rows:]).astype(f32)
        return moves.scatter_mp(total.reshape(rows, mp_count, half))

    parts = {0: experts(0, normed)}
    ahead = behind = normed
    for s in range(1, moves.left + 1):
        ahead = moves.step(ahead, 1)
        parts[-s % moves.chips] = experts(-s, ahead)
        if s <= moves.right:
            behind = moves.step(behind, -1)
            parts[s] = experts(s, behind)

    mixture = parts[0]
    for way, count in ((1, moves.left), (-1, moves.right)):
        carried = None
        for s in range(count, 0, -1):
            part = parts[way * s % moves.chips]
            if carried is not None:
                part = part + carried.astype(f32)
            carried = moves.step(part.astype(bf16), way)
        if carried is not None:
            mixture = mixture + carried.astype(f32)

    own_hidden = lax.dynamic_index_in_dim(
        hidden.reshape(rows, mp_count, half), moves.mp, 1, False
    )
    final = (own_hidden.astype(f32) + mixture).astype(bf16)
    final_float = final.astype(f32)
    final_squares = lax.psum(jnp.sum(final_float * final_float, axis=1), "mp")
    next_normed = (
        final_float * lax.rsqrt(final_squares / D + EPSILON)[:, None] * next_gain
    ).astype(bf16)
    return (final, next_normed)


def solution(mesh):
    in_specs = (
        P("dp", "mp"),
        P("dp", "mp"),
        P("mp", "dp"),
        P("mp"),
        P("dp", "mp"),
        P("dp", "mp"),
        P("mp", "dp"),
        P("dp", None, "mp"),
        P("dp", None, "mp"),
        P("dp", "mp", None),
        P("dp", None),
        P("dp", None),
        P(),
        P("mp"),
    )
    out_specs = (P("dp", "mp"), P("dp", "mp"))
    return jax.shard_map(local, mesh=mesh, in_specs=in_specs, out_specs=out_specs, check_vma=False)
```

```python
import functools

import jax
import jax.numpy as jnp
from jax import lax
from jax.experimental import pallas as pl
from jax.experimental.pallas import tpu as pltpu
from jax.sharding import PartitionSpec as P

D = 2048
EPSILON = 1e-06
CORES = 2
LANES = 128


def matmul(left, right):
    return jnp.dot(left, right, preferred_element_type=jnp.float32)


def chip_cycle(deep, wide):
    if deep == 1 or wide == 1:
        return list(range(deep * wide))
    walk = []
    for y in range(wide):
        line = range(1, deep) if y % 2 == 0 else range(deep - 1, 0, -1)
        walk += [z * wide + y for z in line]
    return walk + list(range(wide - 1, -1, -1))


class Moves:
    def __init__(self, dp_count, mp_count):
        self.chips = dp_count // CORES
        self.mp_count = mp_count
        wide = mp_count if self.chips % mp_count == 0 else 1
        self.cycle = chip_cycle(self.chips // wide, wide)
        self.place = [0] * self.chips
        for at, chip in enumerate(self.cycle):
            self.place[chip] = at
        self.left = self.chips // 2
        self.right = (self.chips - 1) // 2
        self.chip = lax.axis_index("dp") // CORES
        self.core = lax.axis_index("dp") % CORES
        self.mp = lax.axis_index("mp")
        self.at = jnp.asarray(self.place, jnp.int32)[self.chip]

    def step(self, value, way):
        count = self.chips
        pairs = [
            (self.cycle[i] * CORES + c, self.cycle[(i + way) % count] * CORES + c)
            for i in range(count)
            for c in range(CORES)
        ]
        return lax.ppermute(value, "dp", pairs)

    def swap_core(self, value):
        count = self.chips * CORES
        return lax.ppermute(value, "dp", [(d, d ^ 1) for d in range(count)])

    def from_mp(self, value, k):
        count = self.mp_count
        return lax.ppermute(value, "mp", [((i + k) % count, i) for i in range(count)])

    def chip_at(self, offset):
        return jnp.asarray(self.cycle, jnp.int32)[(self.at + offset) % self.chips]

    def gather_mp(self, value):
        whole = jnp.zeros((self.mp_count,) + value.shape, value.dtype)
        whole = lax.dynamic_update_index_in_dim(whole, value, self.mp, 0)
        for k in range(1, self.mp_count):
            whole = lax.dynamic_update_index_in_dim(
                whole, self.from_mp(value, k), (self.mp + k) % self.mp_count, 0
            )
        return whole

    def sum_mp(self, value):
        sent = value.astype(jnp.bfloat16)
        total = sent.astype(jnp.float32)
        for k in range(1, self.mp_count):
            total = total + self.from_mp(sent, k).astype(jnp.float32)
        return total

def round_up(count, multiple):
    return -(-count // multiple) * multiple


def ffn_kernel(blocks, mp_count, mp_ref, score_ref, *refs):
    tokens, refs = refs[:blocks], refs[blocks:]
    stored, refs = refs[:9], refs[9:]
    outs, refs = refs[:mp_count], refs[mp_count:]
    held, (rows_ref, act_ref, shared_act_ref, sems) = refs[:9], refs[9:]
    copies = [pltpu.make_async_copy(stored[i], held[i], sems.at[i]) for i in range(9)]
    for copy in copies:
        copy.start()
    rows = tokens[0].shape[0]
    for i, token_ref in enumerate(tokens):
        rows_ref[pl.ds(i * rows, rows), :] = token_ref[...]
    for e in range(2):
        copies[2 * e].wait()
        gate = matmul(rows_ref[...], held[2 * e][...])
        copies[2 * e + 1].wait()
        up = matmul(rows_ref[...], held[2 * e + 1][...])
        act = gate / (1.0 + jnp.exp(-gate)) * up * score_ref[:, e : e + 1]
        act_ref[e] = act.astype(act_ref.dtype)
    transposed = (((1,), (1,)), ((), ()))
    copies[4].wait()
    copies[5].wait()
    gate = lax.dot_general(
        rows_ref[...], held[4][...], transposed, preferred_element_type=jnp.float32
    )
    up = lax.dot_general(
        rows_ref[...], held[5][...], transposed, preferred_element_type=jnp.float32
    )
    act = gate / (1.0 + jnp.exp(-gate)) * up
    shared_act_ref[...] = act.astype(shared_act_ref.dtype)
    for i in range(6, 9):
        copies[i].wait()
    half = outs[0].shape[1]
    width = 256 if half % 256 == 0 else half
    for k in range(mp_count):
        start = lax.rem(mp_ref[0] + k, mp_count) * half

        def columns(j, carry, k=k, start=start):
            at = pl.ds(pl.multiple_of(start + j * width, LANES), width)
            total = matmul(act_ref[0], held[6][:, at])
            total += matmul(act_ref[1], held[7][:, at])
            total += matmul(shared_act_ref[...], held[8][:, at])
            to = pl.ds(pl.multiple_of(j * width, LANES), width)
            outs[k][:, to] = total.astype(outs[k].dtype)
            return carry

        lax.fori_loop(0, half // width, columns, 0)


def ffn(tokens, score, weights, mp_index, mp_count):
    rows, width = tokens[0].shape
    total = rows * len(tokens)
    half = width // mp_count
    vmem = pl.BlockSpec(memory_space=pltpu.VMEM)
    hidden_units = weights[0].shape[1]
    return pl.pallas_call(
        functools.partial(ffn_kernel, len(tokens), mp_count),
        out_shape=[
            jax.ShapeDtypeStruct((total, half), jnp.float32 if k == 0 else jnp.bfloat16)
            for k in range(mp_count)
        ],
        in_specs=[pl.BlockSpec(memory_space=pltpu.SMEM)]
        + [vmem] * (1 + len(tokens))
        + [pl.BlockSpec(memory_space=pl.ANY)] * len(weights),
        out_specs=[vmem] * mp_count,
        scratch_shapes=[pltpu.VMEM(w.shape, w.dtype) for w in weights]
        + [
            pltpu.VMEM((total, width), jnp.bfloat16),
            pltpu.VMEM((2, total, hidden_units), jnp.bfloat16),
            pltpu.VMEM((total, weights[4].shape[0]), jnp.bfloat16),
            pltpu.SemaphoreType.DMA((len(weights),)),
        ],
        compiler_params=pltpu.CompilerParams(vmem_limit_bytes=48 * 2**20),
        cost_estimate=pl.CostEstimate(
            flops=2 * total * sum(w.size for w in weights),
            bytes_accessed=2 * sum(w.size for w in weights),
            transcendentals=0,
        ),
    )(mp_index, score, *tokens, *weights)


def local(
    attention,
    residual,
    out_weight,
    ffn_gain,
    shared_gate,
    shared_up,
    shared_down,
    expert_gate,
    expert_up,
    expert_down,
    route_ids,
    route_scores,
    placement,
    next_gain,
):
    rows, half = attention.shape
    mp_count = lax.axis_size("mp")
    dp_count = lax.axis_size("dp")
    moves = Moves(dp_count, mp_count)
    chips = moves.chips
    bf16, f32 = jnp.bfloat16, jnp.float32

    both = jnp.concatenate([attention, moves.swap_core(attention)], axis=0)
    whole_residual = moves.gather_mp(residual).transpose(1, 0, 2).reshape(rows, D)
    gain = moves.gather_mp(ffn_gain).reshape(D)
    sums = jnp.zeros((chips, CORES * rows, out_weight.shape[1]), f32)

    def project(sums, blocks):
        values = jnp.stack([matmul(both, w) for _, w in blocks])
        values = moves.sum_mp(values)
        for i, (offset, _) in enumerate(blocks):
            sums = lax.dynamic_update_index_in_dim(sums, values[i], moves.chip_at(offset), 0)
        return sums

    sums = project(sums, [(0, out_weight)])
    ahead = behind = out_weight
    for s in range(1, moves.left + 1):
        ahead = moves.step(ahead, 1)
        blocks = [(-s, ahead)]
        if s <= moves.right:
            behind = moves.step(behind, -1)
            blocks.append((s, behind))
        sums = project(sums, blocks)
        if s == 1:
            first_in = ahead
    mine = sums[:, :rows]
    other = moves.swap_core(sums[:, rows:])
    first = jnp.where(moves.core == 0, mine, other)
    second = jnp.where(moves.core == 0, other, mine)
    projected = jnp.stack([first, second], axis=1).transpose(2, 0, 1, 3).reshape(rows, D)
    hidden = (whole_residual.astype(f32) + projected).astype(bf16)
    hidden_float = hidden.astype(f32)
    squares = jnp.sum(hidden_float * hidden_float, axis=1, keepdims=True)
    normed = (hidden_float * lax.rsqrt(squares / D + EPSILON) * gain).astype(bf16)

    mine = [expert_gate[0], expert_up[0], expert_down[0]]
    other = [moves.swap_core(w) for w in mine]

    units = shared_gate.shape[1] // dp_count
    wide = shared_gate.shape[0]
    shared = jnp.concatenate(
        [
            shared_gate.T.reshape(dp_count, units, wide),
            shared_up.T.reshape(dp_count, units, wide),
            shared_down.reshape(dp_count, units, wide),
        ],
        axis=1,
    )
    shared, _ = lax.optimization_barrier((shared, first_in))
    shared = lax.all_to_all(shared, "dp", 0, 0, tiled=True)
    shared = shared.transpose(1, 0, 2).reshape(3, units, D)
    shared = jnp.concatenate([shared, moves.swap_core(shared)], axis=1)
    spare = round_up(CORES * units, 16) - CORES * units
    shared = jnp.pad(shared, ((0, 0), (0, spare), (0, 0)))
    weights = [
        mine[0], mine[1], other[0], other[1], shared[0], shared[1], mine[2], other[2], shared[2]
    ]

    ids, weight = route_ids.T, route_scores.T
    stored = jnp.arange(dp_count, dtype=jnp.int32)
    expert_of = jnp.sum(
        jnp.where(placement[None, :] == stored[:, None], stored[None, :], 0), axis=1
    )
    own_scores = jnp.sum(
        jnp.where(ids[None] == expert_of[:, None, None], weight[None], 0.0), axis=1
    )
    groups = [list(range(c, dp_count, CORES)) for c in range(CORES)]
    scores = lax.all_to_all(
        own_scores.reshape(chips, CORES, rows), "dp", 0, 0, axis_index_groups=groups, tiled=True
    )
    scores = scores.transpose(0, 2, 1)
    scores = jnp.where(moves.core == 0, scores, scores[..., ::-1])

    mp_index = moves.mp.reshape(1)
    parts = {}

    def experts(blocks):
        score = jnp.concatenate(
            [lax.dynamic_index_in_dim(scores, moves.chip_at(o), 0, False) for o, _ in blocks]
        )
        outs = ffn([b for _, b in blocks], score, weights, mp_index, mp_count)
        total = outs[0]
        for k in range(1, mp_count):
            total = total + moves.from_mp(outs[k], mp_count - k).astype(f32)
        for i, (offset, _) in enumerate(blocks):
            parts[offset % chips] = total[i * rows : (i + 1) * rows]

    blocks = [(0, normed)]
    ahead = behind = normed
    for s in range(1, moves.left + 1):
        ahead = moves.step(ahead, 1)
        blocks.append((-s, ahead))
        if s <= moves.right:
            behind = moves.step(behind, -1)
            blocks.append((s, behind))
        experts(blocks)
        blocks = []

    mixture = parts[0]
    for way, count in ((1, moves.left), (-1, moves.right)):
        carried = None
        for s in range(count, 0, -1):
            part = parts[way * s % chips]
            if carried is not None:
                part = part + carried.astype(f32)
            carried = moves.step(part.astype(bf16), way)
        if carried is not None:
            mixture = mixture + carried.astype(f32)

    own_hidden = lax.dynamic_slice_in_dim(hidden, moves.mp * half, half, 1)
    final = (own_hidden.astype(f32) + mixture).astype(bf16)
    final_float = final.astype(f32)
    final_squares = lax.psum(jnp.sum(final_float * final_float, axis=1), "mp")
    next_normed = (
        final_float * lax.rsqrt(final_squares / D + EPSILON)[:, None] * next_gain
    ).astype(bf16)
    return (final, next_normed)


def solution(mesh):
    in_specs = (
        P("dp", "mp"),
        P("dp", "mp"),
        P("mp", "dp"),
        P("mp"),
        P("dp", "mp"),
        P("dp", "mp"),
        P("mp", "dp"),
        P("dp", None, "mp"),
        P("dp", None, "mp"),
        P("dp", "mp", None),
        P("dp", None),
        P("dp", None),
        P(),
        P("mp"),
    )
    out_specs = (P("dp", "mp"), P("dp", "mp"))
    return jax.shard_map(local, mesh=mesh, in_specs=in_specs, out_specs=out_specs, check_vma=False)
```

```python
import functools

import jax
import jax.numpy as jnp
import numpy as np
from jax import lax
from jax.experimental import pallas as pl
from jax.experimental.pallas import tpu as pltpu
from jax.sharding import PartitionSpec as P

D = 2048
EPSILON = 1e-06
CORES = 2
LANES = 128
VMEM_BYTES = 8 * 2**20
FFN_VMEM = 16 * 2**20


def matmul(left, right):
    return jnp.dot(left, right, preferred_element_type=jnp.float32)


def matmul_nt(left, right):
    return lax.dot_general(
        left, right, (((1,), (1,)), ((), ())), preferred_element_type=jnp.float32
    )


def round_up(count, multiple):
    return -(-count // multiple) * multiple


def chip_cycle(deep, wide):
    if deep == 1 or wide == 1:
        return list(range(deep * wide))
    walk = []
    for y in range(wide):
        line = range(1, deep) if y % 2 == 0 else range(deep - 1, 0, -1)
        walk += [z * wide + y for z in line]
    return walk + list(range(wide - 1, -1, -1))


class Moves:
    def __init__(self, dp_count, mp_count):
        self.chips = dp_count // CORES
        self.mp_count = mp_count
        wide = mp_count if self.chips % mp_count == 0 else 1
        self.cycle = chip_cycle(self.chips // wide, wide)
        self.left = self.chips // 2
        self.right = (self.chips - 1) // 2

    def info(self):
        table = np.zeros((self.chips * CORES, self.mp_count, self.chips + 2), np.int32)
        for at, chip in enumerate(self.cycle):
            for core in range(CORES):
                row = table[chip * CORES + core]
                row[:, : self.chips] = np.roll(self.cycle, -at)
                row[:, self.chips] = core
                row[:, self.chips + 1] = np.arange(self.mp_count)
        return jnp.asarray(table)[lax.axis_index("dp"), lax.axis_index("mp")]

    def step(self, value, way):
        count = self.chips
        pairs = [
            (self.cycle[i] * CORES + c, self.cycle[(i + way) % count] * CORES + c)
            for i in range(count)
            for c in range(CORES)
        ]
        return lax.ppermute(value, "dp", pairs)

    def gather(self, values):
        ahead = [[value] for value in values]
        behind = [[value] for value in values]
        for s in range(1, self.left + 1):
            moved = [self.step(a[-1], 1) for a in ahead]
            if s <= self.right:
                moved += [self.step(b[-1], -1) for b in behind]
            moved = lax.optimization_barrier(moved)
            for a, value in zip(ahead, moved):
                a.append(value)
            for b, value in zip(behind, moved[len(values) :]):
                b.append(value)
        return list(zip(ahead, behind))

    def swap_core(self, value):
        count = self.chips * CORES
        return lax.ppermute(value, "dp", [(d, d ^ 1) for d in range(count)])

    def from_mp(self, value, k):
        count = self.mp_count
        return lax.ppermute(value, "mp", [((i + k) % count, i) for i in range(count)])

    def all_mp(self, value):
        return [value] + [self.from_mp(value, k) for k in range(1, self.mp_count)]


def after(value, *others):
    return lax.optimization_barrier((value, *others))[0]


def vmem():
    return pl.BlockSpec(memory_space=pltpu.VMEM)


def smem():
    return pl.BlockSpec(memory_space=pltpu.SMEM)


def params(*held):
    size = 0
    for shape, dtype in held:
        lanes = round_up(shape[-1], LANES)
        size += np.prod(shape[:-1], dtype=np.int64) * lanes * jnp.dtype(dtype).itemsize
    return pltpu.CompilerParams(vmem_limit_bytes=max(VMEM_BYTES, 2 * int(size)))


def project_kernel(at, blocks, *refs):
    left_ref, other_ref = refs[:2]
    out_ref, other_out_ref = refs[-2:]
    for i in range(blocks):
        block = refs[2 + i][...]
        out_ref[at + i] = matmul(left_ref[...], block).astype(out_ref.dtype)
        other_out_ref[at + i] = matmul(other_ref[...], block).astype(out_ref.dtype)


def project(left, other, blocks, at, into):
    fresh = isinstance(into, int)
    shape = (into if fresh else into[0].shape[0], left.shape[0], blocks[0].shape[1])
    given = [] if fresh else list(into)
    first = 2 + len(blocks)
    return pl.pallas_call(
        functools.partial(project_kernel, at, len(blocks)),
        out_shape=[jax.ShapeDtypeStruct(shape, jnp.bfloat16)] * 2,
        in_specs=[vmem()] * (first + len(given)),
        out_specs=[vmem()] * 2,
        input_output_aliases={first + i: i for i in range(len(given))},
        compiler_params=params(),
        cost_estimate=pl.CostEstimate(
            flops=4 * left.size * shape[2] * len(blocks),
            bytes_accessed=2 * blocks[0].size * len(blocks),
            transcendentals=0,
        ),
    )(left, other, *blocks, *given)


def norm_kernel(offsets, mp_count, info_ref, *refs):
    stacks, refs = refs[: len(offsets) * mp_count], refs[len(offsets) * mp_count :]
    residuals, refs = refs[:mp_count], refs[mp_count:]
    gains, refs = refs[:mp_count], refs[mp_count:]
    normed_ref, own_ref, sums_ref, rest_ref, gain_ref, hidden_ref, sems, *held = refs
    copies = [
        pltpu.make_async_copy(stack, to, sems.at[i])
        for i, (stack, to) in enumerate(zip(stacks, held))
    ]
    for copy in copies:
        copy.start()
    chips = sums_ref.shape[0] // CORES
    core, mp = info_ref[chips], info_ref[chips + 1]
    for s, listed in enumerate(offsets):
        for k in range(mp_count):
            copies[s * mp_count + k].wait()
        for i, (offset, other) in enumerate(listed):
            total = held[s * mp_count][i].astype(jnp.float32)
            for k in range(1, mp_count):
                total = total + held[s * mp_count + k][i].astype(jnp.float32)
            lane = 1 - core if other else core
            sums_ref[info_ref[offset % chips] * CORES + lane] = total
    for k in range(mp_count):
        at = lax.rem(mp + k, mp_count)
        rest_ref[at] = residuals[k][...]
        gain_ref[at] = gains[k][...]
    rows, half = own_ref.shape
    width = sums_ref.shape[2]
    per_half = half // width
    squares = jnp.zeros((rows, 1), jnp.float32)
    for k in range(mp_count):
        pieces = [sums_ref[k * per_half + j] for j in range(per_half)]
        total = rest_ref[k].astype(jnp.float32) + jnp.concatenate(pieces, axis=1)
        hidden = total.astype(jnp.bfloat16).astype(jnp.float32)
        hidden_ref[k] = hidden
        squares += jnp.sum(hidden * hidden, axis=1, keepdims=True)
    scale = lax.rsqrt(squares / (half * mp_count) + EPSILON)
    for k in range(mp_count):
        value = hidden_ref[k] * scale * gain_ref[k]
        normed_ref[:, k * half : (k + 1) * half] = value.astype(normed_ref.dtype)
    own_ref[...] = hidden_ref[mp].astype(own_ref.dtype)


def norm(info, offsets, stacks, residuals, gains):
    mp_count = len(residuals)
    rows, half = residuals[0].shape
    width = stacks[0].shape[2]
    count = half * mp_count // width
    return pl.pallas_call(
        functools.partial(norm_kernel, offsets, mp_count),
        out_shape=[
            jax.ShapeDtypeStruct((rows, half * mp_count), jnp.bfloat16),
            jax.ShapeDtypeStruct((rows, half), jnp.bfloat16),
        ],
        in_specs=[smem()]
        + [pl.BlockSpec(memory_space=pl.ANY)] * len(stacks)
        + [vmem()] * (2 * mp_count),
        out_specs=[vmem()] * 2,
        scratch_shapes=[
            pltpu.VMEM((count, rows, width), jnp.float32),
            pltpu.VMEM((mp_count, rows, half), jnp.bfloat16),
            pltpu.VMEM((mp_count, 1, half), jnp.float32),
            pltpu.VMEM((mp_count, rows, half), jnp.float32),
            pltpu.SemaphoreType.DMA((len(stacks),)),
        ]
        + [pltpu.VMEM(stack.shape, stack.dtype) for stack in stacks],
        compiler_params=params(
            ((count, rows, width), jnp.float32), *[(stack.shape, stack.dtype) for stack in stacks]
        ),
    )(info, *stacks, *residuals, *gains)


def ffn_kernel(offsets, pieces, mp_count, info_ref, *refs):
    scores, refs = refs[:2], refs[2:]
    tokens, refs = refs[:pieces], refs[pieces:]
    held, refs = refs[:9], refs[9:]
    outs, (rows_ref, act_ref, shared_act_ref) = refs[:mp_count], refs[mp_count:]
    at = 0
    for token_ref in tokens:
        rows_ref[pl.ds(at, token_ref.shape[0]), :] = token_ref[...]
        at += token_ref.shape[0]
    chips = info_ref.shape[0] - 2
    turned = []
    for e in range(2):
        devices = [info_ref[offset % chips] * CORES + info_ref[chips] for offset in offsets]
        wide = [scores[e][pl.ds(device, 1), :] for device in devices]
        wide = jnp.broadcast_to(jnp.concatenate(wide, axis=1), (8, at))
        turned.append(wide.T[:, :1])
    for e in range(3):
        gate = matmul_nt(rows_ref[...], held[2 * e][...])
        up = matmul_nt(rows_ref[...], held[2 * e + 1][...])
        act = gate / (1.0 + jnp.exp(-gate)) * up
        if e < 2:
            act_ref[e] = (act * turned[e]).astype(act_ref.dtype)
        else:
            shared_act_ref[...] = act.astype(shared_act_ref.dtype)
    half = outs[0].shape[1]
    width = 256 if half % 256 == 0 else half
    mp = info_ref[info_ref.shape[0] - 1]
    for k in range(mp_count):
        start = lax.rem(mp + k, mp_count) * half

        def columns(j, carry, k=k, start=start):
            at = pl.ds(pl.multiple_of(start + j * width, LANES), width)
            total = matmul(act_ref[0], held[6][:, at])
            total += matmul(act_ref[1], held[7][:, at])
            total += matmul(shared_act_ref[...], held[8][:, at])
            to = pl.ds(pl.multiple_of(j * width, LANES), width)
            outs[k][:, to] = total.astype(outs[k].dtype)
            return carry

        lax.fori_loop(0, half // width, columns, 0)


def ffn(offsets, tokens, scores, weights, info, mp_count):
    width = tokens[0].shape[1]
    total = sum(piece.shape[0] for piece in tokens)
    half = width // mp_count
    hidden_units = weights[0].shape[0]
    return pl.pallas_call(
        functools.partial(ffn_kernel, offsets, len(tokens), mp_count),
        out_shape=[
            jax.ShapeDtypeStruct((total, half), jnp.float32 if k == 0 else jnp.bfloat16)
            for k in range(mp_count)
        ],
        in_specs=[smem()] + [vmem()] * (2 + len(tokens) + len(weights)),
        out_specs=[vmem()] * mp_count,
        scratch_shapes=[
            pltpu.VMEM((total, width), jnp.bfloat16),
            pltpu.VMEM((2, total, hidden_units), jnp.bfloat16),
            pltpu.VMEM((total, weights[4].shape[0]), jnp.bfloat16),
        ],
        compiler_params=pltpu.CompilerParams(vmem_limit_bytes=FFN_VMEM),
        cost_estimate=pl.CostEstimate(
            flops=2 * total * sum(w.size for w in weights),
            bytes_accessed=2 * sum(w.size for w in weights),
            transcendentals=0,
        ),
    )(info, *scores, *tokens, *weights)


def local(
    attention,
    residual,
    out_weight,
    ffn_gain,
    shared_gate,
    shared_up,
    shared_down,
    expert_gate,
    expert_up,
    expert_down,
    route_ids,
    route_scores,
    placement,
    next_gain,
):
    rows, half = attention.shape
    mp_count = lax.axis_size("mp")
    dp_count = lax.axis_size("dp")
    moves = Moves(dp_count, mp_count)
    chips, left, right = moves.chips, moves.left, moves.right
    bf16, f32 = jnp.bfloat16, jnp.float32
    info = moves.info()
    core = info[chips]

    ids, weight = route_ids.T, route_scores.T
    stored = jnp.arange(dp_count, dtype=jnp.int32)
    expert_of = jnp.sum(
        jnp.where(placement[None, :] == stored[:, None], stored[None, :], 0), axis=1
    )
    own_scores = jnp.sum(
        jnp.where(ids[None] == expert_of[:, None, None], weight[None], 0.0), axis=1
    )

    units = shared_gate.shape[1] // dp_count
    wide = shared_gate.shape[0]
    dealt = [
        shared_gate.T.reshape(dp_count, units, wide),
        shared_up.T.reshape(dp_count, units, wide),
        shared_down.reshape(dp_count, units, wide),
    ]
    rest = own_scores
    thirds = []
    for _ in range(3):
        third = lax.reduce_precision(rest, 8, 7)
        thirds.append(third.astype(bf16))
        rest = rest - third
    thirds = jnp.stack(thirds, axis=1).reshape(dp_count, 3 * rows // wide, wide)
    used = 3 * units + thirds.shape[1]
    shared, at = 0, 0
    for part in (*dealt, thirds):
        over = round_up(used, 16) - at - part.shape[1]
        shared = shared + jnp.pad(part, ((0, 0), (at, over), (0, 0)))
        at += part.shape[1]
    mine = [expert_gate[0].T, expert_up[0].T, expert_down[0]]
    other = [moves.swap_core(w) for w in mine]
    other_attention = moves.swap_core(attention)
    residuals = moves.all_mp(residual)
    gains = moves.all_mp(ffn_gain.reshape(1, half))
    offsets, stacks, swapped = [], [], []

    def exchange(listed, own, beside):
        swapped.append(moves.swap_core(beside))
        for value, flip in ((own, False), (swapped[-1], True)):
            offsets.append([(offset, flip) for offset in listed])
            stacks.append(moves.all_mp(value))

    early = 1 + 2 * (left - 1)
    listed, filled = [0], 0
    sums = early
    arrived = [out_weight]
    ahead = behind = out_weight
    for s in range(1, left + 1):
        if s > 1:
            sums = project(attention, other_attention, arrived, filled, sums)
            filled += len(arrived)
            arrived = []
        if s == left:
            exchange(listed, *sums)
            listed = []
        moved = [moves.step(ahead, 1)]
        if s <= right:
            moved.append(moves.step(behind, -1))
        ties = []
        if s == left - 1:
            ties = [shared, *other]
        if s == left:
            ties = [*residuals[1:], *gains[1:]]
        if s > 1:
            ties += sums
        moved, ties = lax.optimization_barrier((moved, ties))
        if s > 1:
            sums = ties[-2:]
        if s == left - 1:
            shared, *other = ties[:-2]
        ahead = moved[0]
        arrived.append(ahead)
        listed.append(-s)
        if s <= right:
            behind = moved[1]
            arrived.append(behind)
            listed.append(s)
    shared = lax.all_to_all(after(shared, swapped[0]), "dp", 0, 0, tiled=True)
    exchange(listed, *project(attention, other_attention, arrived, 0, len(arrived)))
    normed, own_hidden = norm(
        info, offsets, [piece for stack in stacks for piece in stack], residuals, gains
    )
    shared = shared.transpose(1, 0, 2)
    shared = [shared, moves.swap_core(shared)]
    spare = round_up(CORES * units, 16) - CORES * units
    parts = []
    for i in range(3):
        part = [value[i * units : (i + 1) * units].reshape(units, D) for value in shared]
        parts.append(jnp.pad(jnp.concatenate(part), ((0, spare), (0, 0))))
    weights = [
        mine[0], mine[1], other[0], other[1], parts[0], parts[1], mine[2], other[2], parts[2]
    ]
    scores = []
    for value in shared:
        thirds = value[3 * units : used].transpose(1, 0, 2).reshape(dp_count, 3, rows)
        scores.append(jnp.sum(thirds.astype(f32), axis=1))

    def swap_mp(sent):
        return [moves.from_mp(sent[k - 1], mp_count - k) for k in range(1, mp_count)]

    ahead = behind = normed
    listed, blocks = [0], [normed]
    done = []
    for s in range(1, left + 1):
        kept, *sent = ffn(listed, blocks, scores, weights, info, mp_count)
        if s <= right:
            moved = [moves.step(ahead, 1), moves.step(behind, -1)]
        else:
            moved = [moves.step(ahead[: rows // 2], 1), moves.step(behind[rows // 2 :], -1)]
        came = done[-1][2] if done else []
        moved, sent, came = lax.optimization_barrier((moved, sent, came))
        if done:
            done[-1][2] = came
        done.append([listed, kept, swap_mp(sent)])
        ahead, behind = blocks = moved
        listed = [-s, s] if s <= right else [s]
    kept, *sent = ffn(listed, blocks, scores, weights, info, mp_count)
    done.append([listed, kept, swap_mp(sent)])
    parts = {}
    for listed, kept, came in done:
        for value in came:
            kept = kept + value.astype(f32)
        for i, offset in enumerate(listed):
            parts[offset % chips] = kept[i * rows : (i + 1) * rows]

    mixture = parts[0]
    if left > right:
        mixture = mixture + moves.step(parts[left].astype(bf16), left).astype(f32)
    for way in (1, -1):
        carried = None
        for s in range(right, 0, -1):
            part = parts[way * s % chips]
            if carried is not None:
                part = part + carried.astype(f32)
            carried = moves.step(part.astype(bf16), way)
        if carried is not None:
            mixture = mixture + carried.astype(f32)

    final = (own_hidden.astype(f32) + mixture).astype(bf16)
    final_float = final.astype(f32)
    final_squares = lax.psum(jnp.sum(final_float * final_float, axis=1), "mp")
    next_normed = (
        final_float * lax.rsqrt(final_squares / D + EPSILON)[:, None] * next_gain
    ).astype(bf16)
    return (final, next_normed)


def solution(mesh):
    in_specs = (
        P("dp", "mp"),
        P("dp", "mp"),
        P("mp", "dp"),
        P("mp"),
        P("dp", "mp"),
        P("dp", "mp"),
        P("mp", "dp"),
        P("dp", None, "mp"),
        P("dp", None, "mp"),
        P("dp", "mp", None),
        P("dp", None),
        P("dp", None),
        P(),
        P("mp"),
    )
    out_specs = (P("dp", "mp"), P("dp", "mp"))
    return jax.shard_map(local, mesh=mesh, in_specs=in_specs, out_specs=out_specs, check_vma=False)
```

```python
import functools

import jax
import jax.numpy as jnp
import numpy as np
from jax import lax
from jax.experimental import pallas as pl
from jax.experimental.pallas import tpu as pltpu
from jax.sharding import PartitionSpec as P

D = 2048
EPSILON = 1e-06
CORES = 2
LANES = 128
VMEM_BYTES = 8 * 2**20
FFN_VMEM = 28 * 2**20


def matmul(left, right):
    return jnp.dot(left, right, preferred_element_type=jnp.float32)


def matmul_nt(left, right):
    return lax.dot_general(
        left, right, (((1,), (1,)), ((), ())), preferred_element_type=jnp.float32
    )


def round_up(count, multiple):
    return -(-count // multiple) * multiple


def chip_cycle(deep, wide):
    if deep == 1 or wide == 1:
        return list(range(deep * wide))
    walk = []
    for y in range(wide):
        line = range(1, deep) if y % 2 == 0 else range(deep - 1, 0, -1)
        walk += [z * wide + y for z in line]
    return walk + list(range(wide - 1, -1, -1))


class Moves:
    def __init__(self, dp_count, mp_count):
        self.chips = dp_count // CORES
        self.mp_count = mp_count
        wide = mp_count if self.chips % mp_count == 0 else 1
        self.cycle = chip_cycle(self.chips // wide, wide)
        self.left = self.chips // 2
        self.right = (self.chips - 1) // 2

    def info(self):
        table = np.zeros((self.chips * CORES, self.mp_count, self.chips + 2), np.int32)
        for at, chip in enumerate(self.cycle):
            for core in range(CORES):
                row = table[chip * CORES + core]
                row[:, : self.chips] = np.roll(self.cycle, -at)
                row[:, self.chips] = core
                row[:, self.chips + 1] = np.arange(self.mp_count)
        return jnp.asarray(table)[lax.axis_index("dp"), lax.axis_index("mp")]

    def step(self, value, way):
        count = self.chips
        pairs = [
            (self.cycle[i] * CORES + c, self.cycle[(i + way) % count] * CORES + c)
            for i in range(count)
            for c in range(CORES)
        ]
        return lax.ppermute(value, "dp", pairs)

    def gather(self, values):
        ahead = [[value] for value in values]
        behind = [[value] for value in values]
        for s in range(1, self.left + 1):
            moved = [self.step(a[-1], 1) for a in ahead]
            if s <= self.right:
                moved += [self.step(b[-1], -1) for b in behind]
            moved = lax.optimization_barrier(moved)
            for a, value in zip(ahead, moved):
                a.append(value)
            for b, value in zip(behind, moved[len(values) :]):
                b.append(value)
        return list(zip(ahead, behind))

    def step_across(self, value, way, k):
        count = self.chips
        pairs = [
            (
                (self.cycle[i] * CORES + c) * self.mp_count + m,
                (self.cycle[(i + way) % count] * CORES + c) * self.mp_count
                + (m + k) % self.mp_count,
            )
            for i in range(count)
            for c in range(CORES)
            for m in range(self.mp_count)
        ]
        return lax.ppermute(value, ("dp", "mp"), pairs)

    def swap_core(self, value):
        count = self.chips * CORES
        return lax.ppermute(value, "dp", [(d, d ^ 1) for d in range(count)])

    def from_mp(self, value, k):
        count = self.mp_count
        return lax.ppermute(value, "mp", [((i + k) % count, i) for i in range(count)])

    def all_mp(self, value):
        return [value] + [self.from_mp(value, k) for k in range(1, self.mp_count)]


def after(value, *others):
    return lax.optimization_barrier((value, *others))[0]


def vmem():
    return pl.BlockSpec(memory_space=pltpu.VMEM)


def smem():
    return pl.BlockSpec(memory_space=pltpu.SMEM)


def params(*held):
    size = 0
    for shape, dtype in held:
        lanes = round_up(shape[-1], LANES)
        size += np.prod(shape[:-1], dtype=np.int64) * lanes * jnp.dtype(dtype).itemsize
    return pltpu.CompilerParams(vmem_limit_bytes=max(VMEM_BYTES, 2 * int(size)))


def brief():
    return pl.CostEstimate(flops=1, bytes_accessed=1, transcendentals=0)


def project_kernel(at, blocks, *refs):
    left_ref, other_ref = refs[:2]
    out_ref, other_out_ref = refs[-2:]
    for i in range(blocks):
        block = refs[2 + i][...]
        out_ref[at + i] = matmul(left_ref[...], block).astype(out_ref.dtype)
        other_out_ref[at + i] = matmul(other_ref[...], block).astype(out_ref.dtype)


def project(left, other, blocks, at, into):
    fresh = isinstance(into, int)
    shape = (into if fresh else into[0].shape[0], left.shape[0], blocks[0].shape[1])
    given = [] if fresh else list(into)
    first = 2 + len(blocks)
    return pl.pallas_call(
        functools.partial(project_kernel, at, len(blocks)),
        out_shape=[jax.ShapeDtypeStruct(shape, jnp.bfloat16)] * 2,
        in_specs=[vmem()] * (first + len(given)),
        out_specs=[vmem()] * 2,
        input_output_aliases={first + i: i for i in range(len(given))},
        compiler_params=params(),
        cost_estimate=brief(),
    )(left, other, *blocks, *given)


def deal_kernel(gate_ref, up_ref, down_ref, thirds_ref, out_ref):
    count = out_ref.shape[0]
    units = down_ref.shape[0] // count
    gate = gate_ref[...].astype(jnp.float32).T
    up = up_ref[...].astype(jnp.float32).T
    down = down_ref[...].astype(jnp.float32)
    for i in range(count):
        at = slice(i * units, (i + 1) * units)
        listed = [gate[at], up[at], down[at], thirds_ref[i]]
        out_ref[i] = jnp.concatenate(listed, axis=0).astype(out_ref.dtype)


def deal(gate, up, down, thirds):
    count, extra, wide = thirds.shape
    units = down.shape[0] // count
    rows = 3 * units + extra
    if units % 8 or extra % 8 or rows % 16 or wide % LANES:
        parts = [part.reshape(count, units, wide) for part in (gate.T, up.T, down)]
        return jnp.concatenate([*parts, thirds.astype(gate.dtype)], axis=1)
    return pl.pallas_call(
        deal_kernel,
        out_shape=jax.ShapeDtypeStruct((count, rows, wide), gate.dtype),
        in_specs=[vmem()] * 4,
        out_specs=vmem(),
        compiler_params=params(*[((4 * gate.shape[1], wide), jnp.float32)]),
        cost_estimate=brief(),
    )(gate, up, down, thirds)


def norm_kernel(offsets, mp_count, info_ref, *refs):
    stacks, refs = refs[: len(offsets) * mp_count], refs[len(offsets) * mp_count :]
    residuals, refs = refs[:mp_count], refs[mp_count:]
    gains, refs = refs[:mp_count], refs[mp_count:]
    normed_ref, own_ref, sums_ref, rest_ref, gain_ref, hidden_ref, sems, *held = refs
    copies = [
        pltpu.make_async_copy(stack, to, sems.at[i])
        for i, (stack, to) in enumerate(zip(stacks, held))
    ]
    for copy in copies:
        copy.start()
    chips = sums_ref.shape[0] // CORES
    core, mp = info_ref[chips], info_ref[chips + 1]
    for s, listed in enumerate(offsets):
        for k in range(mp_count):
            copies[s * mp_count + k].wait()
        for i, (offset, other) in enumerate(listed):
            total = held[s * mp_count][i].astype(jnp.float32)
            for k in range(1, mp_count):
                total = total + held[s * mp_count + k][i].astype(jnp.float32)
            lane = 1 - core if other else core
            sums_ref[info_ref[offset % chips] * CORES + lane] = total
    for k in range(mp_count):
        at = lax.rem(mp + k, mp_count)
        rest_ref[at] = residuals[k][...]
        gain_ref[at] = gains[k][...]
    rows, half = own_ref.shape
    width = sums_ref.shape[2]
    per_half = half // width
    squares = jnp.zeros((rows, 1), jnp.float32)
    for k in range(mp_count):
        pieces = [sums_ref[k * per_half + j] for j in range(per_half)]
        total = rest_ref[k].astype(jnp.float32) + jnp.concatenate(pieces, axis=1)
        hidden = total.astype(jnp.bfloat16).astype(jnp.float32)
        hidden_ref[k] = hidden
        squares += jnp.sum(hidden * hidden, axis=1, keepdims=True)
    scale = lax.rsqrt(squares / (half * mp_count) + EPSILON)
    for k in range(mp_count):
        value = hidden_ref[k] * scale * gain_ref[k]
        normed_ref[:, k * half : (k + 1) * half] = value.astype(normed_ref.dtype)
    own_ref[...] = hidden_ref[mp].astype(own_ref.dtype)


def norm(info, offsets, stacks, residuals, gains):
    mp_count = len(residuals)
    rows, half = residuals[0].shape
    width = stacks[0].shape[2]
    count = half * mp_count // width
    return pl.pallas_call(
        functools.partial(norm_kernel, offsets, mp_count),
        out_shape=[
            jax.ShapeDtypeStruct((rows, half * mp_count), jnp.bfloat16),
            jax.ShapeDtypeStruct((rows, half), jnp.bfloat16),
        ],
        in_specs=[smem()]
        + [pl.BlockSpec(memory_space=pl.ANY)] * len(stacks)
        + [vmem()] * (2 * mp_count),
        out_specs=[vmem()] * 2,
        scratch_shapes=[
            pltpu.VMEM((count, rows, width), jnp.float32),
            pltpu.VMEM((mp_count, rows, half), jnp.bfloat16),
            pltpu.VMEM((mp_count, 1, half), jnp.float32),
            pltpu.VMEM((mp_count, rows, half), jnp.float32),
            pltpu.SemaphoreType.DMA((len(stacks),)),
        ]
        + [pltpu.VMEM(stack.shape, stack.dtype) for stack in stacks],
        compiler_params=params(
            ((count, rows, width), jnp.float32), *[(stack.shape, stack.dtype) for stack in stacks]
        ),
        cost_estimate=brief(),
    )(info, *stacks, *residuals, *gains)


def ffn_kernel(offsets, pieces, mp_count, info_ref, *refs):
    scores, refs = refs[:2], refs[2:]
    tokens, refs = refs[:pieces], refs[pieces:]
    near, far, refs = refs[:6], refs[6:9], refs[9:]
    outs, refs = refs[:mp_count], refs[mp_count:]
    rows_ref, act_ref, shared_act_ref, sems, *held = refs
    copies = [pltpu.make_async_copy(far[i], held[i], sems.at[i]) for i in range(3)]
    for copy in copies:
        copy.start()
    at = 0
    for token_ref in tokens:
        rows_ref[pl.ds(at, token_ref.shape[0]), :] = token_ref[...]
        at += token_ref.shape[0]
    chips = info_ref.shape[0] - 2
    turned = []
    for e in range(2):
        devices = [info_ref[offset % chips] * CORES + info_ref[chips] for offset in offsets]
        wide = [scores[e][pl.ds(device, 1), :] for device in devices]
        wide = jnp.broadcast_to(jnp.concatenate(wide, axis=1), (8, at))
        turned.append(wide.T[:, :1])
    for gate_ref, up_ref, e in ((near[0], near[1], 0), (near[3], near[4], None), (*held[:2], 1)):
        if e == 1:
            copies[0].wait()
            copies[1].wait()
        gate = matmul_nt(rows_ref[...], gate_ref[...])
        up = matmul_nt(rows_ref[...], up_ref[...])
        act = gate / (1.0 + jnp.exp(-gate)) * up
        if e is None:
            shared_act_ref[...] = act.astype(shared_act_ref.dtype)
        else:
            act_ref[e] = (act * turned[e]).astype(act_ref.dtype)
    copies[2].wait()
    half = outs[0].shape[1]
    width = 256 if half % 256 == 0 else half
    mp = info_ref[info_ref.shape[0] - 1]
    for k in range(mp_count):
        start = lax.rem(mp + k, mp_count) * half

        for j in range(half // width):
            at = pl.ds(pl.multiple_of(start + j * width, LANES), width)
            total = matmul(act_ref[0], near[2][:, at])
            total += matmul(act_ref[1], held[2][:, at])
            total += matmul(shared_act_ref[...], near[5][:, at])
            outs[k][:, j * width : (j + 1) * width] = total.astype(outs[k].dtype)


def ffn(offsets, tokens, scores, weights, info, mp_count):
    width = tokens[0].shape[1]
    total = sum(piece.shape[0] for piece in tokens)
    half = width // mp_count
    hidden_units = weights[0].shape[0]
    return pl.pallas_call(
        functools.partial(ffn_kernel, offsets, len(tokens), mp_count),
        out_shape=[
            jax.ShapeDtypeStruct((total, half), jnp.float32 if k == 0 else jnp.bfloat16)
            for k in range(mp_count)
        ],
        in_specs=[smem()]
        + [vmem()] * (2 + len(tokens) + 6)
        + [pl.BlockSpec(memory_space=pl.ANY)] * 3,
        out_specs=[vmem()] * mp_count,
        scratch_shapes=[
            pltpu.VMEM((total, width), jnp.bfloat16),
            pltpu.VMEM((2, total, hidden_units), jnp.bfloat16),
            pltpu.VMEM((total, weights[3].shape[0]), jnp.bfloat16),
            pltpu.SemaphoreType.DMA((3,)),
        ]
        + [pltpu.VMEM(w.shape, w.dtype) for w in weights[6:]],
        compiler_params=pltpu.CompilerParams(vmem_limit_bytes=FFN_VMEM),
        cost_estimate=brief(),
    )(info, *scores, *tokens, *weights)


def local(
    attention,
    residual,
    out_weight,
    ffn_gain,
    shared_gate,
    shared_up,
    shared_down,
    expert_gate,
    expert_up,
    expert_down,
    route_ids,
    route_scores,
    placement,
    next_gain,
):
    rows, half = attention.shape
    mp_count = lax.axis_size("mp")
    dp_count = lax.axis_size("dp")
    moves = Moves(dp_count, mp_count)
    chips, left, right = moves.chips, moves.left, moves.right
    bf16, f32 = jnp.bfloat16, jnp.float32
    info = moves.info()
    core = info[chips]

    ids, weight = route_ids.T, route_scores.T
    stored = jnp.arange(dp_count, dtype=jnp.int32)
    expert_of = jnp.sum(
        jnp.where(placement[None, :] == stored[:, None], stored[None, :], 0), axis=1
    )
    own_scores = jnp.sum(
        jnp.where(ids[None] == expert_of[:, None, None], weight[None], 0.0), axis=1
    )

    units = shared_gate.shape[1] // dp_count
    wide = shared_gate.shape[0]
    rest = own_scores
    thirds = []
    for _ in range(3):
        thirds.append(lax.reduce_precision(rest, 8, 7))
        rest = rest - thirds[-1]
    thirds = jnp.stack(thirds, axis=1).reshape(dp_count, 3 * rows // wide, wide)
    used = 3 * units + thirds.shape[1]
    thirds = jnp.pad(thirds, ((0, 0), (0, round_up(used, 16) - used), (0, 0)))
    shared = deal(shared_gate, shared_up, shared_down, thirds)

    mine = [expert_gate[0].T, expert_up[0].T, expert_down[0]]
    other_attention = moves.swap_core(attention)
    residuals = moves.all_mp(residual)
    gains = moves.all_mp(ffn_gain.reshape(1, half))
    offsets, stacks, swapped = [], [], []

    def exchange(listed, own, beside):
        swapped.append(moves.swap_core(beside))
        for value, flip in ((own, False), (swapped[-1], True)):
            offsets.append([(offset, flip) for offset in listed])
            stacks.append(moves.all_mp(value))

    early = 1 + 2 * (left - 1)
    listed, filled = [0], 0
    sums = early
    arrived = [out_weight]
    ahead = behind = out_weight
    for s in range(1, left + 1):
        if s > 1:
            sums = project(attention, other_attention, arrived, filled, sums)
            filled += len(arrived)
            arrived = []
        if s == left:
            exchange(listed, *sums)
            listed = []
        moved = [moves.step(ahead, 1)]
        if s <= right:
            moved.append(moves.step(behind, -1))
        ties = []
        if s == left - 1:
            ties = [shared, *residuals[1:], *gains[1:]]
        if s > 1:
            ties += sums
        moved, ties = lax.optimization_barrier((moved, ties))
        if s > 1:
            sums = ties[-2:]
        if s == left - 1:
            shared = ties[0]
        ahead = moved[0]
        arrived.append(ahead)
        listed.append(-s)
        if s <= right:
            behind = moved[1]
            arrived.append(behind)
            listed.append(s)
    shared = lax.all_to_all(after(shared, ahead, stacks[0][-1]), "dp", 0, 0, tiled=True)
    other = [moves.swap_core(after(w, ahead)) for w in mine]
    exchange(listed, *project(attention, other_attention, arrived, 0, len(arrived)))
    normed, own_hidden = norm(
        info, offsets, [piece for stack in stacks for piece in stack], residuals, gains
    )
    shared = shared.transpose(1, 0, 2)
    shared = [shared, moves.swap_core(shared)]
    spare = round_up(CORES * units, 16) - CORES * units
    parts = []
    for i in range(3):
        part = [value[i * units : (i + 1) * units].reshape(units, D) for value in shared]
        parts.append(jnp.pad(jnp.concatenate(part), ((0, spare), (0, 0))))
    weights = [*mine, *parts, *other]
    scores = []
    for value in shared:
        thirds = value[3 * units : used].transpose(1, 0, 2).reshape(dp_count, 3, rows)
        scores.append(jnp.sum(thirds.astype(f32), axis=1))

    def swap_mp(sent):
        return [moves.from_mp(sent[k - 1], mp_count - k) for k in range(1, mp_count)]

    ahead = behind = normed
    listed, blocks = [0], [normed]
    done = []
    for s in range(1, left + 1):
        outs = list(ffn(listed, blocks, scores, weights, info, mp_count))
        done.append([listed, outs, None])
        if s <= right:
            moved = [moves.step(ahead, 1), moves.step(behind, -1)]
        else:
            moved = [moves.step(ahead[: rows // 2], 1), moves.step(behind[rows // 2 :], -1)]
        came = done[-2][2] if s >= 2 else []
        moved, ties, came = lax.optimization_barrier((moved, outs[1:], came))
        if s >= 2:
            done[-2][2] = came
        done[-1][2] = swap_mp(ties)
        ahead, behind = blocks = moved
        listed = [-s, s] if s <= right else [s]
    done.append([listed, ffn(listed, blocks, scores, weights, info, mp_count), None])
    parts, whole = {}, {}
    for listed, (kept, *sent), came in done:
        if right in listed:
            for i, offset in enumerate(listed):
                whole[offset] = [value[i * rows : (i + 1) * rows] for value in (kept, *sent)]
            continue
        for value in swap_mp(sent) if came is None else came:
            kept = kept + value.astype(f32)
        for i, offset in enumerate(listed):
            parts[offset] = kept[i * rows : (i + 1) * rows]

    carried = []
    for way in (1, -1):
        kept, *sent = whole[way * right]
        came = [moves.step(kept.astype(bf16), way)]
        came += [moves.step_across(value, way, k + 1) for k, value in enumerate(sent)]
        for s in range(right - 1, 0, -1):
            part = parts[way * s]
            for value in came:
                part = part + value.astype(f32)
            came = [moves.step(part.astype(bf16), way)]
        carried += came
    mixture = parts[0]
    if left > right:
        carried.append(moves.step(parts[left].astype(bf16), left))
    for value in carried:
        mixture = mixture + value.astype(f32)

    final = (own_hidden.astype(f32) + mixture).astype(bf16)
    final_float = final.astype(f32)
    final_squares = lax.psum(jnp.sum(final_float * final_float, axis=1), "mp")
    next_normed = (
        final_float * lax.rsqrt(final_squares / D + EPSILON)[:, None] * next_gain
    ).astype(bf16)
    return (final, next_normed)


def solution(mesh):
    in_specs = (
        P("dp", "mp"),
        P("dp", "mp"),
        P("mp", "dp"),
        P("mp"),
        P("dp", "mp"),
        P("dp", "mp"),
        P("mp", "dp"),
        P("dp", None, "mp"),
        P("dp", None, "mp"),
        P("dp", "mp", None),
        P("dp", None),
        P("dp", None),
        P(),
        P("mp"),
    )
    out_specs = (P("dp", "mp"), P("dp", "mp"))
    return jax.shard_map(local, mesh=mesh, in_specs=in_specs, out_specs=out_specs, check_vma=False)
```

```python
import functools

import jax
import jax.numpy as jnp
import numpy as np
from jax import lax
from jax.experimental import pallas as pl
from jax.experimental.pallas import tpu as pltpu
from jax.sharding import PartitionSpec as P

D = 2048
EPSILON = 1e-06
CORES = 2
LANES = 128
VMEM_BYTES = 8 * 2**20
FFN_VMEM = 28 * 2**20


def matmul(left, right):
    return jnp.dot(left, right, preferred_element_type=jnp.float32)


def matmul_nt(left, right):
    return lax.dot_general(
        left, right, (((1,), (1,)), ((), ())), preferred_element_type=jnp.float32
    )


def round_up(count, multiple):
    return -(-count // multiple) * multiple


def chip_cycle(deep, wide):
    if deep == 1 or wide == 1:
        return list(range(deep * wide))
    walk = []
    for y in range(wide):
        line = range(1, deep) if y % 2 == 0 else range(deep - 1, 0, -1)
        walk += [z * wide + y for z in line]
    return walk + list(range(wide - 1, -1, -1))


class Moves:
    def __init__(self, dp_count, mp_count):
        self.chips = dp_count // CORES
        self.mp_count = mp_count
        wide = mp_count if self.chips % mp_count == 0 else 1
        self.cycle = chip_cycle(self.chips // wide, wide)
        self.left = self.chips // 2
        self.right = (self.chips - 1) // 2

    def info(self):
        table = np.zeros((self.chips * CORES, self.mp_count, self.chips + 2), np.int32)
        for at, chip in enumerate(self.cycle):
            for core in range(CORES):
                row = table[chip * CORES + core]
                row[:, : self.chips] = np.roll(self.cycle, -at)
                row[:, self.chips] = core
                row[:, self.chips + 1] = np.arange(self.mp_count)
        return jnp.asarray(table)[lax.axis_index("dp"), lax.axis_index("mp")]

    def step(self, value, way):
        count = self.chips
        pairs = [
            (self.cycle[i] * CORES + c, self.cycle[(i + way) % count] * CORES + c)
            for i in range(count)
            for c in range(CORES)
        ]
        return lax.ppermute(value, "dp", pairs)

    def gather(self, values):
        ahead = [[value] for value in values]
        behind = [[value] for value in values]
        for s in range(1, self.left + 1):
            moved = [self.step(a[-1], 1) for a in ahead]
            if s <= self.right:
                moved += [self.step(b[-1], -1) for b in behind]
            moved = lax.optimization_barrier(moved)
            for a, value in zip(ahead, moved):
                a.append(value)
            for b, value in zip(behind, moved[len(values) :]):
                b.append(value)
        return list(zip(ahead, behind))

    def step_across(self, value, way, k):
        count = self.chips
        pairs = [
            (
                (self.cycle[i] * CORES + c) * self.mp_count + m,
                (self.cycle[(i + way) % count] * CORES + c) * self.mp_count
                + (m + k) % self.mp_count,
            )
            for i in range(count)
            for c in range(CORES)
            for m in range(self.mp_count)
        ]
        return lax.ppermute(value, ("dp", "mp"), pairs)

    def swap_core(self, value):
        count = self.chips * CORES
        return lax.ppermute(value, "dp", [(d, d ^ 1) for d in range(count)])

    def from_mp(self, value, k):
        count = self.mp_count
        return lax.ppermute(value, "mp", [((i + k) % count, i) for i in range(count)])

    def all_mp(self, value):
        return [value] + [self.from_mp(value, k) for k in range(1, self.mp_count)]


def after(value, *others):
    return lax.optimization_barrier((value, *others))[0]


def vmem():
    return pl.BlockSpec(memory_space=pltpu.VMEM)


def smem():
    return pl.BlockSpec(memory_space=pltpu.SMEM)


def params(*held):
    size = 0
    for shape, dtype in held:
        lanes = round_up(shape[-1], LANES)
        size += np.prod(shape[:-1], dtype=np.int64) * lanes * jnp.dtype(dtype).itemsize
    return pltpu.CompilerParams(vmem_limit_bytes=max(VMEM_BYTES, 2 * int(size)))


def brief():
    return pl.CostEstimate(flops=1, bytes_accessed=1, transcendentals=0)


def project_kernel(at, blocks, *refs):
    left_ref, other_ref = refs[:2]
    out_ref, other_out_ref = refs[-2:]
    for i in range(blocks):
        block = refs[2 + i][...]
        out_ref[at + i] = matmul(left_ref[...], block).astype(out_ref.dtype)
        other_out_ref[at + i] = matmul(other_ref[...], block).astype(out_ref.dtype)


def project(left, other, blocks, at, into):
    fresh = isinstance(into, int)
    shape = (into if fresh else into[0].shape[0], left.shape[0], blocks[0].shape[1])
    given = [] if fresh else list(into)
    first = 2 + len(blocks)
    return pl.pallas_call(
        functools.partial(project_kernel, at, len(blocks)),
        out_shape=[jax.ShapeDtypeStruct(shape, jnp.bfloat16)] * 2,
        in_specs=[vmem()] * (first + len(given)),
        out_specs=[vmem()] * 2,
        input_output_aliases={first + i: i for i in range(len(given))},
        compiler_params=params(),
        cost_estimate=brief(),
    )(left, other, *blocks, *given)


def deal_kernel(gate_ref, up_ref, down_ref, thirds_ref, out_ref):
    count = out_ref.shape[0]
    units = down_ref.shape[0] // count
    gate = gate_ref[...].astype(jnp.float32).T
    up = up_ref[...].astype(jnp.float32).T
    down = down_ref[...].astype(jnp.float32)
    for i in range(count):
        at = slice(i * units, (i + 1) * units)
        listed = [gate[at], up[at], down[at], thirds_ref[i]]
        out_ref[i] = jnp.concatenate(listed, axis=0).astype(out_ref.dtype)


def deal(gate, up, down, thirds):
    count, extra, wide = thirds.shape
    units = down.shape[0] // count
    rows = 3 * units + extra
    if units % 8 or extra % 8 or rows % 16 or wide % LANES:
        parts = [part.reshape(count, units, wide) for part in (gate.T, up.T, down)]
        return jnp.concatenate([*parts, thirds.astype(gate.dtype)], axis=1)
    return pl.pallas_call(
        deal_kernel,
        out_shape=jax.ShapeDtypeStruct((count, rows, wide), gate.dtype),
        in_specs=[vmem()] * 4,
        out_specs=vmem(),
        compiler_params=params(*[((4 * gate.shape[1], wide), jnp.float32)]),
        cost_estimate=brief(),
    )(gate, up, down, thirds)


def norm_kernel(offsets, mp_count, info_ref, *refs):
    stacks, refs = refs[: len(offsets) * mp_count], refs[len(offsets) * mp_count :]
    residuals, refs = refs[:mp_count], refs[mp_count:]
    gains, refs = refs[:mp_count], refs[mp_count:]
    normed_ref, own_ref, sums_ref, rest_ref, gain_ref, hidden_ref, sems, *held = refs
    copies = [
        pltpu.make_async_copy(stack, to, sems.at[i])
        for i, (stack, to) in enumerate(zip([*stacks, *residuals], held))
    ]
    for copy in copies:
        copy.start()
    chips = sums_ref.shape[0] // CORES
    core, mp = info_ref[chips], info_ref[chips + 1]
    for s, listed in enumerate(offsets):
        for k in range(mp_count):
            copies[s * mp_count + k].wait()
        for i, (offset, other) in enumerate(listed):
            total = held[s * mp_count][i].astype(jnp.float32)
            for k in range(1, mp_count):
                total = total + held[s * mp_count + k][i].astype(jnp.float32)
            lane = 1 - core if other else core
            sums_ref[info_ref[offset % chips] * CORES + lane] = total
    for k in range(mp_count):
        at = lax.rem(mp + k, mp_count)
        copies[len(stacks) + k].wait()
        rest_ref[at] = held[len(stacks) + k][...]
        gain_ref[at] = gains[k][...]
    rows, half = own_ref.shape
    width = sums_ref.shape[2]
    per_half = half // width
    squares = jnp.zeros((rows, 1), jnp.float32)
    for k in range(mp_count):
        pieces = [sums_ref[k * per_half + j] for j in range(per_half)]
        total = rest_ref[k].astype(jnp.float32) + jnp.concatenate(pieces, axis=1)
        hidden = total.astype(jnp.bfloat16).astype(jnp.float32)
        hidden_ref[k] = hidden
        squares += jnp.sum(hidden * hidden, axis=1, keepdims=True)
    scale = lax.rsqrt(squares / (half * mp_count) + EPSILON)
    for k in range(mp_count):
        value = hidden_ref[k] * scale * gain_ref[k]
        normed_ref[:, k * half : (k + 1) * half] = value.astype(normed_ref.dtype)
    own_ref[...] = hidden_ref[mp].astype(own_ref.dtype)


def norm(info, offsets, stacks, residuals, gains):
    mp_count = len(residuals)
    rows, half = residuals[0].shape
    width = stacks[0].shape[2]
    count = half * mp_count // width
    return pl.pallas_call(
        functools.partial(norm_kernel, offsets, mp_count),
        out_shape=[
            jax.ShapeDtypeStruct((rows, half * mp_count), jnp.bfloat16),
            jax.ShapeDtypeStruct((rows, half), jnp.bfloat16),
        ],
        in_specs=[smem()]
        + [pl.BlockSpec(memory_space=pl.ANY)] * (len(stacks) + mp_count)
        + [vmem()] * mp_count,
        out_specs=[vmem()] * 2,
        scratch_shapes=[
            pltpu.VMEM((count, rows, width), jnp.float32),
            pltpu.VMEM((mp_count, rows, half), jnp.bfloat16),
            pltpu.VMEM((mp_count, 1, half), jnp.float32),
            pltpu.VMEM((mp_count, rows, half), jnp.float32),
            pltpu.SemaphoreType.DMA((len(stacks) + mp_count,)),
        ]
        + [pltpu.VMEM(value.shape, value.dtype) for value in (*stacks, *residuals)],
        compiler_params=params(
            ((count, rows, width), jnp.float32), *[(stack.shape, stack.dtype) for stack in stacks]
        ),
        cost_estimate=brief(),
    )(info, *stacks, *residuals, *gains)


def ffn_kernel(offsets, pieces, mp_count, info_ref, *refs):
    scores, refs = refs[:2], refs[2:]
    tokens, refs = refs[:pieces], refs[pieces:]
    near, far, refs = refs[:6], refs[6:9], refs[9:]
    outs, refs = refs[:mp_count], refs[mp_count:]
    rows_ref, act_ref, shared_act_ref, sems, *held = refs
    copies = [pltpu.make_async_copy(far[i], held[i], sems.at[i]) for i in range(3)]
    for copy in copies:
        copy.start()
    at = 0
    for token_ref in tokens:
        rows_ref[pl.ds(at, token_ref.shape[0]), :] = token_ref[...]
        at += token_ref.shape[0]
    chips = info_ref.shape[0] - 2
    turned = []
    for e in range(2):
        devices = [info_ref[offset % chips] * CORES + info_ref[chips] for offset in offsets]
        wide = [scores[e][pl.ds(device, 1), :] for device in devices]
        wide = jnp.broadcast_to(jnp.concatenate(wide, axis=1), (8, at))
        turned.append(wide.T[:, :1])
    for gate_ref, up_ref, e in ((near[0], near[1], 0), (near[3], near[4], None), (*held[:2], 1)):
        if e == 1:
            copies[0].wait()
            copies[1].wait()
        gate = matmul_nt(rows_ref[...], gate_ref[...])
        up = matmul_nt(rows_ref[...], up_ref[...])
        act = gate / (1.0 + jnp.exp(-gate)) * up
        if e is None:
            shared_act_ref[...] = act.astype(shared_act_ref.dtype)
        else:
            act_ref[e] = (act * turned[e]).astype(act_ref.dtype)
    copies[2].wait()
    half = outs[0].shape[1]
    width = 256 if half % 256 == 0 else half
    mp = info_ref[info_ref.shape[0] - 1]
    for k in range(mp_count):
        start = lax.rem(mp + k, mp_count) * half

        for j in range(half // width):
            at = pl.ds(pl.multiple_of(start + j * width, LANES), width)
            total = matmul(act_ref[0], near[2][:, at])
            total += matmul(act_ref[1], held[2][:, at])
            total += matmul(shared_act_ref[...], near[5][:, at])
            outs[k][:, j * width : (j + 1) * width] = total.astype(outs[k].dtype)


def ffn(offsets, tokens, scores, weights, info, mp_count):
    width = tokens[0].shape[1]
    total = sum(piece.shape[0] for piece in tokens)
    half = width // mp_count
    hidden_units = weights[0].shape[0]
    return pl.pallas_call(
        functools.partial(ffn_kernel, offsets, len(tokens), mp_count),
        out_shape=[
            jax.ShapeDtypeStruct((total, half), jnp.float32 if k == 0 else jnp.bfloat16)
            for k in range(mp_count)
        ],
        in_specs=[smem()]
        + [vmem()] * (2 + len(tokens) + 6)
        + [pl.BlockSpec(memory_space=pl.ANY)] * 3,
        out_specs=[vmem()] * mp_count,
        scratch_shapes=[
            pltpu.VMEM((total, width), jnp.bfloat16),
            pltpu.VMEM((2, total, hidden_units), jnp.bfloat16),
            pltpu.VMEM((total, weights[3].shape[0]), jnp.bfloat16),
            pltpu.SemaphoreType.DMA((3,)),
        ]
        + [pltpu.VMEM(w.shape, w.dtype) for w in weights[6:]],
        compiler_params=pltpu.CompilerParams(vmem_limit_bytes=FFN_VMEM),
        cost_estimate=brief(),
    )(info, *scores, *tokens, *weights)


def local(
    attention,
    residual,
    out_weight,
    ffn_gain,
    shared_gate,
    shared_up,
    shared_down,
    expert_gate,
    expert_up,
    expert_down,
    route_ids,
    route_scores,
    placement,
    next_gain,
):
    rows, half = attention.shape
    mp_count = lax.axis_size("mp")
    dp_count = lax.axis_size("dp")
    moves = Moves(dp_count, mp_count)
    chips, left, right = moves.chips, moves.left, moves.right
    bf16, f32 = jnp.bfloat16, jnp.float32
    info = moves.info()
    core = info[chips]

    ids, weight = route_ids.T, route_scores.T
    stored = jnp.arange(dp_count, dtype=jnp.int32)
    expert_of = jnp.sum(
        jnp.where(placement[None, :] == stored[:, None], stored[None, :], 0), axis=1
    )
    own_scores = jnp.sum(
        jnp.where(ids[None] == expert_of[:, None, None], weight[None], 0.0), axis=1
    )

    units = shared_gate.shape[1] // dp_count
    wide = shared_gate.shape[0]
    rest = own_scores
    thirds = []
    for _ in range(3):
        thirds.append(lax.reduce_precision(rest, 8, 7))
        rest = rest - thirds[-1]
    thirds = jnp.stack(thirds, axis=1).reshape(dp_count, 3 * rows // wide, wide)
    used = 3 * units + thirds.shape[1]
    thirds = jnp.pad(thirds, ((0, 0), (0, round_up(used, 16) - used), (0, 0)))
    shared = deal(shared_gate, shared_up, shared_down, thirds)

    mine = [expert_gate[0].T, expert_up[0].T, expert_down[0]]
    other_attention = moves.swap_core(attention)
    residuals = moves.all_mp(residual)
    gains = moves.all_mp(ffn_gain.reshape(1, half))
    offsets, stacks, swapped = [], [], []

    def exchange(listed, own, beside):
        swapped.append(moves.swap_core(beside))
        for value, flip in ((own, False), (swapped[-1], True)):
            offsets.append([(offset, flip) for offset in listed])
            stacks.append(moves.all_mp(value))

    early = 1 + 2 * (left - 1)
    listed, filled = [0], 0
    sums = early
    arrived = [out_weight]
    ahead = behind = out_weight
    for s in range(1, left + 1):
        if s > 1:
            sums = project(attention, other_attention, arrived, filled, sums)
            filled += len(arrived)
            arrived = []
        if s == left:
            exchange(listed, *sums)
            listed = []
        moved = [moves.step(ahead, 1)]
        if s <= right:
            moved.append(moves.step(behind, -1))
        ties = []
        if s == left - 1:
            ties = [shared, *residuals[1:], *gains[1:]]
        if s > 1:
            ties += sums
        moved, ties = lax.optimization_barrier((moved, ties))
        if s > 1:
            sums = ties[-2:]
        if s == left - 1:
            shared = ties[0]
        ahead = moved[0]
        arrived.append(ahead)
        listed.append(-s)
        if s <= right:
            behind = moved[1]
            arrived.append(behind)
            listed.append(s)
    shared = lax.all_to_all(after(shared, ahead), "dp", 0, 0, tiled=True)
    other = [moves.swap_core(after(w, ahead)) for w in mine]
    exchange(listed, *project(attention, other_attention, arrived, 0, len(arrived)))
    normed, own_hidden = norm(
        info, offsets, [piece for stack in stacks for piece in stack], residuals, gains
    )
    shared = after(shared, normed).transpose(1, 0, 2)
    shared = [shared, moves.swap_core(shared)]

    def unpack(shared):
        spare = round_up(CORES * units, 16) - CORES * units
        parts = []
        for i in range(3):
            part = [value[i * units : (i + 1) * units].reshape(units, D) for value in shared]
            parts.append(jnp.pad(jnp.concatenate(part), ((0, spare), (0, 0))))
        weights = [*mine, *parts, *other]
        scores = []
        for value in shared:
            thirds = value[3 * units : used].transpose(1, 0, 2).reshape(dp_count, 3, rows)
            scores.append(jnp.sum(thirds.astype(f32), axis=1))
        return weights, scores

    def swap_mp(sent):
        return [moves.from_mp(sent[k - 1], mp_count - k) for k in range(1, mp_count)]

    ahead = behind = normed
    done = []
    for s in range(1, left + 1):
        if s > 1:
            outs = list(ffn(listed, blocks, scores, weights, info, mp_count))
            done.append([listed, outs, None])
        if s <= right:
            moved = [moves.step(ahead, 1), moves.step(behind, -1)]
        else:
            moved = [moves.step(ahead[: rows // 2], 1), moves.step(behind[rows // 2 :], -1)]
        if s > 1:
            came = done[-2][2] if s > 2 else []
            moved, ties, came = lax.optimization_barrier((moved, outs[1:], came))
            if s > 2:
                done[-2][2] = came
            done[-1][2] = swap_mp(ties)
        else:
            moved, shared = lax.optimization_barrier((moved, shared))
            weights, scores = unpack(shared)
        ahead, behind = blocks = moved
        listed = [-s, s] if s <= right else [s]
    outs = ffn([*listed, 0], [*blocks, normed], scores, weights, info, mp_count)
    for start, stop, offsets in (
        (0, rows * len(listed), listed),
        (rows * len(listed), rows * (len(listed) + 1), [0]),
    ):
        done.append([offsets, [value[start:stop] for value in outs], None])
    parts, whole = {}, {}
    for listed, (kept, *sent), came in done:
        if right in listed:
            for i, offset in enumerate(listed):
                whole[offset] = [value[i * rows : (i + 1) * rows] for value in (kept, *sent)]
            continue
        for value in swap_mp(sent) if came is None else came:
            kept = kept + value.astype(f32)
        for i, offset in enumerate(listed):
            parts[offset] = kept[i * rows : (i + 1) * rows]

    carried = []
    for way in (1, -1):
        kept, *sent = whole[way * right]
        came = [moves.step(kept.astype(bf16), way)]
        came += [moves.step_across(value, way, k + 1) for k, value in enumerate(sent)]
        for s in range(right - 1, 0, -1):
            part = parts[way * s]
            for value in came:
                part = part + value.astype(f32)
            came = [moves.step(part.astype(bf16), way)]
        carried += came
    mixture = parts[0]
    if left > right:
        carried.append(moves.step(parts[left].astype(bf16), left))
    for value in carried:
        mixture = mixture + value.astype(f32)

    final = (own_hidden.astype(f32) + mixture).astype(bf16)
    final_float = final.astype(f32)
    squares = moves.all_mp(jnp.sum(final_float * final_float, axis=1, keepdims=True).T)
    scale = lax.rsqrt(sum(squares) / D + EPSILON).T
    next_normed = (final_float * scale * next_gain).astype(bf16)
    return (final, next_normed)


def solution(mesh):
    in_specs = (
        P("dp", "mp"),
        P("dp", "mp"),
        P("mp", "dp"),
        P("mp"),
        P("dp", "mp"),
        P("dp", "mp"),
        P("mp", "dp"),
        P("dp", None, "mp"),
        P("dp", None, "mp"),
        P("dp", "mp", None),
        P("dp", None),
        P("dp", None),
        P(),
        P("mp"),
    )
    out_specs = (P("dp", "mp"), P("dp", "mp"))
    return jax.shard_map(local, mesh=mesh, in_specs=in_specs, out_specs=out_specs, check_vma=False)
```

```python
import functools

import jax
import jax.numpy as jnp
import numpy as np
from jax import lax
from jax.experimental import pallas as pl
from jax.experimental.pallas import tpu as pltpu
from jax.sharding import PartitionSpec as P

D = 2048
EPSILON = 1e-06
CORES = 2
LANES = 128
VMEM_BYTES = 8 * 2**20
FFN_VMEM = 28 * 2**20


def matmul(left, right):
    return jnp.dot(left, right, preferred_element_type=jnp.float32)


def matmul_nt(left, right):
    return lax.dot_general(
        left, right, (((1,), (1,)), ((), ())), preferred_element_type=jnp.float32
    )


def round_up(count, multiple):
    return -(-count // multiple) * multiple


def chip_cycle(deep, wide):
    if deep == 1 or wide == 1:
        return list(range(deep * wide))
    walk = []
    for y in range(wide):
        line = range(1, deep) if y % 2 == 0 else range(deep - 1, 0, -1)
        walk += [z * wide + y for z in line]
    return walk + list(range(wide - 1, -1, -1))


class Moves:
    def __init__(self, dp_count, mp_count):
        self.chips = dp_count // CORES
        self.mp_count = mp_count
        wide = mp_count if self.chips % mp_count == 0 else 1
        self.cycle = chip_cycle(self.chips // wide, wide)
        self.left = self.chips // 2
        self.right = (self.chips - 1) // 2

    def info(self):
        table = np.zeros((self.chips * CORES, self.mp_count, self.chips + 2), np.int32)
        for at, chip in enumerate(self.cycle):
            for core in range(CORES):
                row = table[chip * CORES + core]
                row[:, : self.chips] = np.roll(self.cycle, -at)
                row[:, self.chips] = core
                row[:, self.chips + 1] = np.arange(self.mp_count)
        return jnp.asarray(table)[lax.axis_index("dp"), lax.axis_index("mp")]

    def step(self, value, way):
        count = self.chips
        pairs = [
            (self.cycle[i] * CORES + c, self.cycle[(i + way) % count] * CORES + c)
            for i in range(count)
            for c in range(CORES)
        ]
        return lax.ppermute(value, "dp", pairs)

    def gather(self, values):
        ahead = [[value] for value in values]
        behind = [[value] for value in values]
        for s in range(1, self.left + 1):
            moved = [self.step(a[-1], 1) for a in ahead]
            if s <= self.right:
                moved += [self.step(b[-1], -1) for b in behind]
            moved = lax.optimization_barrier(moved)
            for a, value in zip(ahead, moved):
                a.append(value)
            for b, value in zip(behind, moved[len(values) :]):
                b.append(value)
        return list(zip(ahead, behind))

    def step_across(self, value, way, k):
        count = self.chips
        pairs = [
            (
                (self.cycle[i] * CORES + c) * self.mp_count + m,
                (self.cycle[(i + way) % count] * CORES + c) * self.mp_count
                + (m + k) % self.mp_count,
            )
            for i in range(count)
            for c in range(CORES)
            for m in range(self.mp_count)
        ]
        return lax.ppermute(value, ("dp", "mp"), pairs)

    def swap_core(self, value):
        count = self.chips * CORES
        return lax.ppermute(value, "dp", [(d, d ^ 1) for d in range(count)])

    def from_mp(self, value, k):
        count = self.mp_count
        return lax.ppermute(value, "mp", [((i + k) % count, i) for i in range(count)])

    def all_mp(self, value):
        return [value] + [self.from_mp(value, k) for k in range(1, self.mp_count)]


def after(value, *others):
    return lax.optimization_barrier((value, *others))[0]


def vmem():
    return pl.BlockSpec(memory_space=pltpu.VMEM)


def smem():
    return pl.BlockSpec(memory_space=pltpu.SMEM)


def params(*held):
    size = 0
    for shape, dtype in held:
        lanes = round_up(shape[-1], LANES)
        size += np.prod(shape[:-1], dtype=np.int64) * lanes * jnp.dtype(dtype).itemsize
    return pltpu.CompilerParams(vmem_limit_bytes=max(VMEM_BYTES, 2 * int(size)))


def brief():
    return pl.CostEstimate(flops=1, bytes_accessed=1, transcendentals=0)


def project_kernel(at, blocks, *refs):
    left_ref, other_ref = refs[:2]
    out_ref, other_out_ref = refs[-2:]
    for i in range(blocks):
        block = refs[2 + i][...]
        out_ref[at + i] = matmul(left_ref[...], block).astype(out_ref.dtype)
        other_out_ref[at + i] = matmul(other_ref[...], block).astype(out_ref.dtype)


def project(left, other, blocks, at, into):
    fresh = isinstance(into, int)
    shape = (into if fresh else into[0].shape[0], left.shape[0], blocks[0].shape[1])
    given = [] if fresh else list(into)
    first = 2 + len(blocks)
    return pl.pallas_call(
        functools.partial(project_kernel, at, len(blocks)),
        out_shape=[jax.ShapeDtypeStruct(shape, jnp.bfloat16)] * 2,
        in_specs=[vmem()] * (first + len(given)),
        out_specs=[vmem()] * 2,
        input_output_aliases={first + i: i for i in range(len(given))},
        compiler_params=params(),
        cost_estimate=brief(),
    )(left, other, *blocks, *given)


def deal_kernel(gate_ref, up_ref, down_ref, thirds_ref, out_ref):
    count = out_ref.shape[0]
    units = down_ref.shape[0] // count
    gate = gate_ref[...].astype(jnp.float32).T
    up = up_ref[...].astype(jnp.float32).T
    down = down_ref[...].astype(jnp.float32)
    for i in range(count):
        at = slice(i * units, (i + 1) * units)
        listed = [gate[at], up[at], down[at], thirds_ref[i]]
        out_ref[i] = jnp.concatenate(listed, axis=0).astype(out_ref.dtype)


def deal(gate, up, down, thirds):
    count, extra, wide = thirds.shape
    units = down.shape[0] // count
    rows = 3 * units + extra
    if units % 8 or extra % 8 or rows % 16 or wide % LANES:
        parts = [part.reshape(count, units, wide) for part in (gate.T, up.T, down)]
        return jnp.concatenate([*parts, thirds.astype(gate.dtype)], axis=1)
    return pl.pallas_call(
        deal_kernel,
        out_shape=jax.ShapeDtypeStruct((count, rows, wide), gate.dtype),
        in_specs=[vmem()] * 4,
        out_specs=vmem(),
        compiler_params=params(*[((4 * gate.shape[1], wide), jnp.float32)]),
        cost_estimate=brief(),
    )(gate, up, down, thirds)


def norm_kernel(offsets, mp_count, info_ref, *refs):
    stacks, refs = refs[: len(offsets) * mp_count], refs[len(offsets) * mp_count :]
    residuals, refs = refs[:mp_count], refs[mp_count:]
    gains, refs = refs[:mp_count], refs[mp_count:]
    normed_ref, own_ref, sums_ref, rest_ref, gain_ref, hidden_ref, sems, *held = refs
    copies = [
        pltpu.make_async_copy(stack, to, sems.at[i])
        for i, (stack, to) in enumerate(zip([*stacks, *residuals], held))
    ]
    for copy in copies:
        copy.start()
    chips = sums_ref.shape[0] // CORES
    core, mp = info_ref[chips], info_ref[chips + 1]
    for s, listed in enumerate(offsets):
        for k in range(mp_count):
            copies[s * mp_count + k].wait()
        for i, (offset, other) in enumerate(listed):
            total = held[s * mp_count][i].astype(jnp.float32)
            for k in range(1, mp_count):
                total = total + held[s * mp_count + k][i].astype(jnp.float32)
            lane = 1 - core if other else core
            sums_ref[info_ref[offset % chips] * CORES + lane] = total
    for k in range(mp_count):
        at = lax.rem(mp + k, mp_count)
        copies[len(stacks) + k].wait()
        rest_ref[at] = held[len(stacks) + k][...]
        gain_ref[at] = gains[k][...]
    rows, half = own_ref.shape
    width = sums_ref.shape[2]
    per_half = half // width
    squares = jnp.zeros((rows, 1), jnp.float32)
    for k in range(mp_count):
        pieces = [sums_ref[k * per_half + j] for j in range(per_half)]
        total = rest_ref[k].astype(jnp.float32) + jnp.concatenate(pieces, axis=1)
        hidden = total.astype(jnp.bfloat16).astype(jnp.float32)
        hidden_ref[k] = hidden
        squares += jnp.sum(hidden * hidden, axis=1, keepdims=True)
    scale = lax.rsqrt(squares / (half * mp_count) + EPSILON)
    for k in range(mp_count):
        value = hidden_ref[k] * scale * gain_ref[k]
        normed_ref[:, k * half : (k + 1) * half] = value.astype(normed_ref.dtype)
    own_ref[...] = hidden_ref[mp].astype(own_ref.dtype)


def norm(info, offsets, stacks, residuals, gains):
    mp_count = len(residuals)
    rows, half = residuals[0].shape
    width = stacks[0].shape[2]
    count = half * mp_count // width
    return pl.pallas_call(
        functools.partial(norm_kernel, offsets, mp_count),
        out_shape=[
            jax.ShapeDtypeStruct((rows, half * mp_count), jnp.bfloat16),
            jax.ShapeDtypeStruct((rows, half), jnp.bfloat16),
        ],
        in_specs=[smem()]
        + [pl.BlockSpec(memory_space=pl.ANY)] * (len(stacks) + mp_count)
        + [vmem()] * mp_count,
        out_specs=[vmem()] * 2,
        scratch_shapes=[
            pltpu.VMEM((count, rows, width), jnp.float32),
            pltpu.VMEM((mp_count, rows, half), jnp.bfloat16),
            pltpu.VMEM((mp_count, 1, half), jnp.float32),
            pltpu.VMEM((mp_count, rows, half), jnp.float32),
            pltpu.SemaphoreType.DMA((len(stacks) + mp_count,)),
        ]
        + [pltpu.VMEM(value.shape, value.dtype) for value in (*stacks, *residuals)],
        compiler_params=params(
            ((count, rows, width), jnp.float32), *[(stack.shape, stack.dtype) for stack in stacks]
        ),
        cost_estimate=brief(),
    )(info, *stacks, *residuals, *gains)


def ffn_kernel(offsets, pieces, mp_count, info_ref, *refs):
    scores, refs = refs[:2], refs[2:]
    tokens, refs = refs[:pieces], refs[pieces:]
    near, far, refs = refs[:6], refs[6:9], refs[9:]
    outs, refs = refs[:mp_count], refs[mp_count:]
    rows_ref, act_ref, shared_act_ref, sems, *held = refs
    copies = [pltpu.make_async_copy(far[i], held[i], sems.at[i]) for i in range(3)]
    for copy in copies:
        copy.start()
    at = 0
    for token_ref in tokens:
        rows_ref[pl.ds(at, token_ref.shape[0]), :] = token_ref[...]
        at += token_ref.shape[0]
    chips = info_ref.shape[0] - 2
    turned = []
    for e in range(2):
        devices = [info_ref[offset % chips] * CORES + info_ref[chips] for offset in offsets]
        wide = [scores[e][pl.ds(device, 1), :] for device in devices]
        wide = jnp.broadcast_to(jnp.concatenate(wide, axis=1), (8, at))
        turned.append(wide.T[:, :1])
    for gate_ref, up_ref, e in ((near[0], near[1], 0), (near[3], near[4], None), (*held[:2], 1)):
        if e == 1:
            copies[0].wait()
            copies[1].wait()
        gate = matmul_nt(rows_ref[...], gate_ref[...])
        up = matmul_nt(rows_ref[...], up_ref[...])
        act = gate / (1.0 + jnp.exp(-gate)) * up
        if e is None:
            shared_act_ref[...] = act.astype(shared_act_ref.dtype)
        else:
            act_ref[e] = (act * turned[e]).astype(act_ref.dtype)
    copies[2].wait()
    half = outs[0].shape[1]
    width = 256 if half % 256 == 0 else half
    mp = info_ref[info_ref.shape[0] - 1]
    for k in range(mp_count):
        start = lax.rem(mp + k, mp_count) * half

        for j in range(half // width):
            at = pl.ds(pl.multiple_of(start + j * width, LANES), width)
            total = matmul(act_ref[0], near[2][:, at])
            total += matmul(act_ref[1], held[2][:, at])
            total += matmul(shared_act_ref[...], near[5][:, at])
            outs[k][:, j * width : (j + 1) * width] = total.astype(outs[k].dtype)


def ffn(offsets, tokens, scores, weights, info, mp_count):
    width = tokens[0].shape[1]
    total = sum(piece.shape[0] for piece in tokens)
    half = width // mp_count
    hidden_units = weights[0].shape[0]
    return pl.pallas_call(
        functools.partial(ffn_kernel, offsets, len(tokens), mp_count),
        out_shape=[
            jax.ShapeDtypeStruct((total, half), jnp.float32 if k == 0 else jnp.bfloat16)
            for k in range(mp_count)
        ],
        in_specs=[smem()]
        + [vmem()] * (2 + len(tokens) + 6)
        + [pl.BlockSpec(memory_space=pl.ANY)] * 3,
        out_specs=[vmem()] * mp_count,
        scratch_shapes=[
            pltpu.VMEM((total, width), jnp.bfloat16),
            pltpu.VMEM((2, total, hidden_units), jnp.bfloat16),
            pltpu.VMEM((total, weights[3].shape[0]), jnp.bfloat16),
            pltpu.SemaphoreType.DMA((3,)),
        ]
        + [pltpu.VMEM(w.shape, w.dtype) for w in weights[6:]],
        compiler_params=pltpu.CompilerParams(vmem_limit_bytes=FFN_VMEM),
        cost_estimate=brief(),
    )(info, *scores, *tokens, *weights)


def local(
    attention,
    residual,
    out_weight,
    ffn_gain,
    shared_gate,
    shared_up,
    shared_down,
    expert_gate,
    expert_up,
    expert_down,
    route_ids,
    route_scores,
    placement,
    next_gain,
):
    rows, half = attention.shape
    mp_count = lax.axis_size("mp")
    dp_count = lax.axis_size("dp")
    moves = Moves(dp_count, mp_count)
    chips, left, right = moves.chips, moves.left, moves.right
    bf16, f32 = jnp.bfloat16, jnp.float32
    info = moves.info()
    core = info[chips]

    ids, weight = route_ids.T, route_scores.T
    stored = jnp.arange(dp_count, dtype=jnp.int32)
    expert_of = jnp.sum(
        jnp.where(placement[None, :] == stored[:, None], stored[None, :], 0), axis=1
    )
    own_scores = jnp.sum(
        jnp.where(ids[None] == expert_of[:, None, None], weight[None], 0.0), axis=1
    )

    units = shared_gate.shape[1] // dp_count
    wide = shared_gate.shape[0]
    rest = own_scores
    thirds = []
    for _ in range(3):
        thirds.append(lax.reduce_precision(rest, 8, 7))
        rest = rest - thirds[-1]
    thirds = jnp.stack(thirds, axis=1).reshape(dp_count, 3 * rows // wide, wide)
    used = 3 * units + thirds.shape[1]
    thirds = jnp.pad(thirds, ((0, 0), (0, round_up(used, 16) - used), (0, 0)))
    shared = deal(shared_gate, shared_up, shared_down, thirds)

    mine = [expert_gate[0].T, expert_up[0].T, expert_down[0]]
    other_attention = moves.swap_core(attention)
    residuals = moves.all_mp(residual)
    gains = moves.all_mp(ffn_gain.reshape(1, half))
    offsets, stacks, swapped = [], [], []

    def exchange(listed, own, beside):
        swapped.append(moves.swap_core(beside))
        for value, flip in ((own, False), (swapped[-1], True)):
            offsets.append([(offset, flip) for offset in listed])
            stacks.append(moves.all_mp(value))

    early = 1 + 2 * (left - 1)
    listed, filled = [0], 0
    sums = early
    arrived = [out_weight]
    ahead = behind = out_weight
    for s in range(1, left + 1):
        if s > 1:
            sums = project(attention, other_attention, arrived, filled, sums)
            filled += len(arrived)
            arrived = []
        if s == left:
            exchange(listed, *sums)
            listed = []
        moved = [moves.step(ahead, 1)]
        if s <= right:
            moved.append(moves.step(behind, -1))
        ties = []
        if s == left - 1:
            ties = [shared, *residuals[1:], *gains[1:]]
        if s > 1:
            ties += sums
        moved, ties = lax.optimization_barrier((moved, ties))
        if s > 1:
            sums = ties[-2:]
        if s == left - 1:
            shared = ties[0]
        ahead = moved[0]
        arrived.append(ahead)
        listed.append(-s)
        if s <= right:
            behind = moved[1]
            arrived.append(behind)
            listed.append(s)
    shared = lax.all_to_all(after(shared, ahead), "dp", 0, 0, tiled=True)
    other = [moves.swap_core(after(w, ahead)) for w in mine]
    exchange(listed, *project(attention, other_attention, arrived, 0, len(arrived)))
    normed, own_hidden = norm(
        info, offsets, [piece for stack in stacks for piece in stack], residuals, gains
    )
    shared = after(shared, normed).transpose(1, 0, 2)
    shared = [shared, moves.swap_core(shared)]

    def unpack(shared):
        spare = round_up(CORES * units, 16) - CORES * units
        parts = []
        for i in range(3):
            part = [value[i * units : (i + 1) * units].reshape(units, D) for value in shared]
            parts.append(jnp.pad(jnp.concatenate(part), ((0, spare), (0, 0))))
        weights = [*mine, *parts, *other]
        scores = []
        for value in shared:
            thirds = value[3 * units : used].transpose(1, 0, 2).reshape(dp_count, 3, rows)
            scores.append(jnp.sum(thirds.astype(f32), axis=1))
        return weights, scores

    def swap_mp(sent):
        return [moves.from_mp(sent[k - 1], mp_count - k) for k in range(1, mp_count)]

    gate = moves.from_mp(normed[:16, :LANES], 1)
    shared = [after(value, gate) for value in shared]
    weights, scores = unpack(shared)
    ahead = behind = normed
    done = []
    for s in range(1, left + 1):
        if s > 1:
            outs = list(ffn(listed, blocks, scores, weights, info, mp_count))
            done.append([listed, outs, None])
        if s <= right:
            moved = [moves.step(ahead, 1), moves.step(behind, -1)]
        else:
            moved = [moves.step(ahead, 1)]
        if s > 1:
            came = done[-2][2] if s > 2 else []
            moved, ties, came = lax.optimization_barrier((moved, outs[1:], came))
            if s > 2:
                done[-2][2] = came
            done[-1][2] = swap_mp(outs[1:])
        else:
            moved, weights[3:6], scores = lax.optimization_barrier((moved, weights[3:6], scores))
        ahead, behind, blocks = moved[0], moved[-1], moved
        listed = [-s, s] if s <= right else [s]
    outs = ffn([*listed, 0], [*blocks, normed], scores, weights, info, mp_count)
    for start, stop, offsets in (
        (0, rows * len(listed), listed),
        (rows * len(listed), rows * (len(listed) + 1), [0]),
    ):
        done.append([offsets, [value[start:stop] for value in outs], None])
    parts, whole = {}, {}
    for listed, (kept, *sent), came in done:
        if right in listed:
            for i, offset in enumerate(listed):
                whole[offset] = [value[i * rows : (i + 1) * rows] for value in (kept, *sent)]
            continue
        for value in swap_mp(sent) if came is None else came:
            kept = kept + value.astype(f32)
        for i, offset in enumerate(listed):
            parts[offset] = kept[i * rows : (i + 1) * rows]

    carried = []
    for way in (1, -1):
        kept, *sent = whole[way * right]
        came = [moves.step(kept.astype(bf16), way)]
        came += [moves.step_across(value, way, k + 1) for k, value in enumerate(sent)]
        for s in range(right - 1, 0, -1):
            part = parts[way * s]
            for value in came:
                part = part + value.astype(f32)
            came = [moves.step(part.astype(bf16), way)]
        carried += came
    mixture = parts[0]
    if left > right:
        carried.append(moves.step(parts[left].astype(bf16), left))
    for value in carried:
        mixture = mixture + value.astype(f32)

    final = (own_hidden.astype(f32) + mixture).astype(bf16)
    final_float = final.astype(f32)
    squares = moves.all_mp(jnp.sum(final_float * final_float, axis=1, keepdims=True).T)
    scale = lax.rsqrt(sum(squares) / D + EPSILON).T
    next_normed = (final_float * scale * next_gain).astype(bf16)
    return (final, next_normed)


def solution(mesh):
    in_specs = (
        P("dp", "mp"),
        P("dp", "mp"),
        P("mp", "dp"),
        P("mp"),
        P("dp", "mp"),
        P("dp", "mp"),
        P("mp", "dp"),
        P("dp", None, "mp"),
        P("dp", None, "mp"),
        P("dp", "mp", None),
        P("dp", None),
        P("dp", None),
        P(),
        P("mp"),
    )
    out_specs = (P("dp", "mp"), P("dp", "mp"))
    return jax.shard_map(local, mesh=mesh, in_specs=in_specs, out_specs=out_specs, check_vma=False)
```

```python
import functools

import jax
import jax.numpy as jnp
import numpy as np
from jax import lax
from jax.experimental import pallas as pl
from jax.experimental.pallas import tpu as pltpu
from jax.sharding import PartitionSpec as P

D = 2048
EPSILON = 1e-06
CORES = 2
LANES = 128
VMEM_BYTES = 8 * 2**20
FFN_VMEM = 20 * 2**20


def matmul(left, right):
    return jnp.dot(left, right, preferred_element_type=jnp.float32)


def matmul_nt(left, right):
    return lax.dot_general(
        left, right, (((1,), (1,)), ((), ())), preferred_element_type=jnp.float32
    )


def round_up(count, multiple):
    return -(-count // multiple) * multiple


def chip_cycle(deep, wide):
    if deep == 1 or wide == 1:
        return list(range(deep * wide))
    walk = []
    for y in range(wide):
        line = range(1, deep) if y % 2 == 0 else range(deep - 1, 0, -1)
        walk += [z * wide + y for z in line]
    return walk + list(range(wide - 1, -1, -1))


class Moves:
    def __init__(self, dp_count, mp_count):
        self.chips = dp_count // CORES
        self.mp_count = mp_count
        wide = mp_count if self.chips % mp_count == 0 else 1
        self.cycle = chip_cycle(self.chips // wide, wide)
        self.left = self.chips // 2
        self.right = (self.chips - 1) // 2

    def info(self):
        table = np.zeros((self.chips * CORES, self.mp_count, self.chips + 2), np.int32)
        for at, chip in enumerate(self.cycle):
            for core in range(CORES):
                row = table[chip * CORES + core]
                row[:, : self.chips] = np.roll(self.cycle, -at)
                row[:, self.chips] = core
                row[:, self.chips + 1] = np.arange(self.mp_count)
        return jnp.asarray(table)[lax.axis_index("dp"), lax.axis_index("mp")]

    def step(self, value, way):
        count = self.chips
        pairs = [
            (self.cycle[i] * CORES + c, self.cycle[(i + way) % count] * CORES + c)
            for i in range(count)
            for c in range(CORES)
        ]
        return lax.ppermute(value, "dp", pairs)

    def gather(self, values):
        ahead = [[value] for value in values]
        behind = [[value] for value in values]
        for s in range(1, self.left + 1):
            moved = [self.step(a[-1], 1) for a in ahead]
            if s <= self.right:
                moved += [self.step(b[-1], -1) for b in behind]
            moved = lax.optimization_barrier(moved)
            for a, value in zip(ahead, moved):
                a.append(value)
            for b, value in zip(behind, moved[len(values) :]):
                b.append(value)
        return list(zip(ahead, behind))

    def step_across(self, value, way, k):
        count = self.chips
        pairs = [
            (
                (self.cycle[i] * CORES + c) * self.mp_count + m,
                (self.cycle[(i + way) % count] * CORES + c) * self.mp_count
                + (m + k) % self.mp_count,
            )
            for i in range(count)
            for c in range(CORES)
            for m in range(self.mp_count)
        ]
        return lax.ppermute(value, ("dp", "mp"), pairs)

    def swap_core(self, value):
        count = self.chips * CORES
        return lax.ppermute(value, "dp", [(d, d ^ 1) for d in range(count)])

    def from_mp(self, value, k):
        count = self.mp_count
        return lax.ppermute(value, "mp", [((i + k) % count, i) for i in range(count)])

    def all_mp(self, value):
        return [value] + [self.from_mp(value, k) for k in range(1, self.mp_count)]


def after(value, *others):
    return lax.optimization_barrier((value, *others))[0]


def vmem():
    return pl.BlockSpec(memory_space=pltpu.VMEM)


def smem():
    return pl.BlockSpec(memory_space=pltpu.SMEM)


def params(*held):
    size = 0
    for shape, dtype in held:
        lanes = round_up(shape[-1], LANES)
        size += np.prod(shape[:-1], dtype=np.int64) * lanes * jnp.dtype(dtype).itemsize
    return pltpu.CompilerParams(vmem_limit_bytes=max(VMEM_BYTES, 2 * int(size)))


def brief():
    return pl.CostEstimate(flops=1, bytes_accessed=1, transcendentals=0)


def project_kernel(at, blocks, *refs):
    left_ref, other_ref = refs[:2]
    out_ref, other_out_ref = refs[-2:]
    for i in range(blocks):
        block = refs[2 + i][...]
        out_ref[at + i] = matmul(left_ref[...], block).astype(out_ref.dtype)
        other_out_ref[at + i] = matmul(other_ref[...], block).astype(out_ref.dtype)


def project(left, other, blocks, at, into):
    fresh = isinstance(into, int)
    shape = (into if fresh else into[0].shape[0], left.shape[0], blocks[0].shape[1])
    given = [] if fresh else list(into)
    first = 2 + len(blocks)
    return pl.pallas_call(
        functools.partial(project_kernel, at, len(blocks)),
        out_shape=[jax.ShapeDtypeStruct(shape, jnp.bfloat16)] * 2,
        in_specs=[vmem()] * (first + len(given)),
        out_specs=[vmem()] * 2,
        input_output_aliases={first + i: i for i in range(len(given))},
        compiler_params=params(),
        cost_estimate=brief(),
    )(left, other, *blocks, *given)


def deal_kernel(gate_ref, up_ref, down_ref, thirds_ref, out_ref):
    count = out_ref.shape[0]
    units = down_ref.shape[0] // count
    gate = gate_ref[...].astype(jnp.float32).T
    up = up_ref[...].astype(jnp.float32).T
    down = down_ref[...].astype(jnp.float32)
    for i in range(count):
        at = slice(i * units, (i + 1) * units)
        listed = [gate[at], up[at], down[at], thirds_ref[i]]
        out_ref[i] = jnp.concatenate(listed, axis=0).astype(out_ref.dtype)


def deal(gate, up, down, thirds):
    count, extra, wide = thirds.shape
    units = down.shape[0] // count
    rows = 3 * units + extra
    if units % 8 or extra % 8 or rows % 16 or wide % LANES:
        parts = [part.reshape(count, units, wide) for part in (gate.T, up.T, down)]
        return jnp.concatenate([*parts, thirds.astype(gate.dtype)], axis=1)
    return pl.pallas_call(
        deal_kernel,
        out_shape=jax.ShapeDtypeStruct((count, rows, wide), gate.dtype),
        in_specs=[vmem()] * 4,
        out_specs=vmem(),
        compiler_params=params(*[((4 * gate.shape[1], wide), jnp.float32)]),
        cost_estimate=brief(),
    )(gate, up, down, thirds)


def norm_kernel(offsets, mp_count, info_ref, *refs):
    stacks, refs = refs[: len(offsets) * mp_count], refs[len(offsets) * mp_count :]
    residuals, refs = refs[:mp_count], refs[mp_count:]
    gains, refs = refs[:mp_count], refs[mp_count:]
    normed_ref, own_ref, sums_ref, rest_ref, gain_ref, hidden_ref, sems, *held = refs
    copies = [
        pltpu.make_async_copy(stack, to, sems.at[i])
        for i, (stack, to) in enumerate(zip([*stacks, *residuals], held))
    ]
    for copy in copies:
        copy.start()
    chips = sums_ref.shape[0] // CORES
    core, mp = info_ref[chips], info_ref[chips + 1]
    for s, listed in enumerate(offsets):
        for k in range(mp_count):
            copies[s * mp_count + k].wait()
        for i, (offset, other) in enumerate(listed):
            total = held[s * mp_count][i].astype(jnp.float32)
            for k in range(1, mp_count):
                total = total + held[s * mp_count + k][i].astype(jnp.float32)
            lane = 1 - core if other else core
            sums_ref[info_ref[offset % chips] * CORES + lane] = total
    for k in range(mp_count):
        at = lax.rem(mp + k, mp_count)
        copies[len(stacks) + k].wait()
        rest_ref[at] = held[len(stacks) + k][...]
        gain_ref[at] = gains[k][...]
    rows, half = own_ref.shape
    width = sums_ref.shape[2]
    per_half = half // width
    squares = jnp.zeros((rows, 1), jnp.float32)
    for k in range(mp_count):
        pieces = [sums_ref[k * per_half + j] for j in range(per_half)]
        total = rest_ref[k].astype(jnp.float32) + jnp.concatenate(pieces, axis=1)
        hidden = total.astype(jnp.bfloat16).astype(jnp.float32)
        hidden_ref[k] = hidden
        squares += jnp.sum(hidden * hidden, axis=1, keepdims=True)
    scale = lax.rsqrt(squares / (half * mp_count) + EPSILON)
    for k in range(mp_count):
        value = hidden_ref[k] * scale * gain_ref[k]
        normed_ref[:, k * half : (k + 1) * half] = value.astype(normed_ref.dtype)
    own_ref[...] = hidden_ref[mp].astype(own_ref.dtype)


def norm(info, offsets, stacks, residuals, gains):
    mp_count = len(residuals)
    rows, half = residuals[0].shape
    width = stacks[0].shape[2]
    count = half * mp_count // width
    return pl.pallas_call(
        functools.partial(norm_kernel, offsets, mp_count),
        out_shape=[
            jax.ShapeDtypeStruct((rows, half * mp_count), jnp.bfloat16),
            jax.ShapeDtypeStruct((rows, half), jnp.bfloat16),
        ],
        in_specs=[smem()]
        + [pl.BlockSpec(memory_space=pl.ANY)] * (len(stacks) + mp_count)
        + [vmem()] * mp_count,
        out_specs=[vmem()] * 2,
        scratch_shapes=[
            pltpu.VMEM((count, rows, width), jnp.float32),
            pltpu.VMEM((mp_count, rows, half), jnp.bfloat16),
            pltpu.VMEM((mp_count, 1, half), jnp.float32),
            pltpu.VMEM((mp_count, rows, half), jnp.float32),
            pltpu.SemaphoreType.DMA((len(stacks) + mp_count,)),
        ]
        + [pltpu.VMEM(value.shape, value.dtype) for value in (*stacks, *residuals)],
        compiler_params=params(
            ((count, rows, width), jnp.float32), *[(stack.shape, stack.dtype) for stack in stacks]
        ),
        cost_estimate=brief(),
    )(info, *stacks, *residuals, *gains)


def ffn_kernel(offsets, pieces, mp_count, info_ref, *refs):
    scores, refs = refs[:2], refs[2:]
    tokens, refs = refs[:pieces], refs[pieces:]
    near, far, refs = refs[:6], refs[6:9], refs[9:]
    outs, refs = refs[:mp_count], refs[mp_count:]
    rows_ref, act_ref, shared_act_ref, sems, *held = refs
    copies = [pltpu.make_async_copy(far[i], held[i], sems.at[i]) for i in range(3)]
    for copy in copies:
        copy.start()
    at = 0
    for token_ref in tokens:
        rows_ref[pl.ds(at, token_ref.shape[0]), :] = token_ref[...]
        at += token_ref.shape[0]
    chips = info_ref.shape[0] - 2
    turned = []
    for e in range(2):
        devices = [info_ref[offset % chips] * CORES + info_ref[chips] for offset in offsets]
        wide = [scores[e][pl.ds(device, 1), :] for device in devices]
        wide = jnp.broadcast_to(jnp.concatenate(wide, axis=1), (8, at))
        turned.append(wide.T[:, :1])
    for gate_ref, up_ref, e in ((near[0], near[1], 0), (near[3], near[4], None), (*held[:2], 1)):
        if e == 1:
            copies[0].wait()
            copies[1].wait()
        gate = matmul_nt(rows_ref[...], gate_ref[...])
        up = matmul_nt(rows_ref[...], up_ref[...])
        act = gate / (1.0 + jnp.exp(-gate)) * up
        if e is None:
            shared_act_ref[...] = act.astype(shared_act_ref.dtype)
        else:
            act_ref[e] = (act * turned[e]).astype(act_ref.dtype)
    copies[2].wait()
    half = outs[0].shape[1]
    width = 256 if half % 256 == 0 else half
    mp = info_ref[info_ref.shape[0] - 1]
    for k in range(mp_count):
        start = lax.rem(mp + k, mp_count) * half

        for j in range(half // width):
            at = pl.ds(pl.multiple_of(start + j * width, LANES), width)
            total = matmul(act_ref[0], near[2][:, at])
            total += matmul(act_ref[1], held[2][:, at])
            total += matmul(shared_act_ref[...], near[5][:, at])
            outs[k][:, j * width : (j + 1) * width] = total.astype(outs[k].dtype)


def ffn(offsets, tokens, scores, weights, info, mp_count):
    width = tokens[0].shape[1]
    total = sum(piece.shape[0] for piece in tokens)
    half = width // mp_count
    hidden_units = weights[0].shape[0]
    return pl.pallas_call(
        functools.partial(ffn_kernel, offsets, len(tokens), mp_count),
        out_shape=[
            jax.ShapeDtypeStruct((total, half), jnp.float32 if k == 0 else jnp.bfloat16)
            for k in range(mp_count)
        ],
        in_specs=[smem()]
        + [vmem()] * (2 + len(tokens) + 6)
        + [pl.BlockSpec(memory_space=pl.ANY)] * 3,
        out_specs=[vmem()] * mp_count,
        scratch_shapes=[
            pltpu.VMEM((total, width), jnp.bfloat16),
            pltpu.VMEM((2, total, hidden_units), jnp.bfloat16),
            pltpu.VMEM((total, weights[3].shape[0]), jnp.bfloat16),
            pltpu.SemaphoreType.DMA((3,)),
        ]
        + [pltpu.VMEM(w.shape, w.dtype) for w in weights[6:]],
        compiler_params=pltpu.CompilerParams(vmem_limit_bytes=FFN_VMEM),
        cost_estimate=brief(),
    )(info, *scores, *tokens, *weights)


def local(
    attention,
    residual,
    out_weight,
    ffn_gain,
    shared_gate,
    shared_up,
    shared_down,
    expert_gate,
    expert_up,
    expert_down,
    route_ids,
    route_scores,
    placement,
    next_gain,
):
    rows, half = attention.shape
    mp_count = lax.axis_size("mp")
    dp_count = lax.axis_size("dp")
    moves = Moves(dp_count, mp_count)
    chips, left, right = moves.chips, moves.left, moves.right
    bf16, f32 = jnp.bfloat16, jnp.float32
    info = moves.info()
    core = info[chips]

    ids, weight = route_ids.T, route_scores.T
    stored = jnp.arange(dp_count, dtype=jnp.int32)
    expert_of = jnp.sum(
        jnp.where(placement[None, :] == stored[:, None], stored[None, :], 0), axis=1
    )
    own_scores = jnp.sum(
        jnp.where(ids[None] == expert_of[:, None, None], weight[None], 0.0), axis=1
    )

    units = shared_gate.shape[1] // dp_count
    wide = shared_gate.shape[0]
    rest = own_scores
    thirds = []
    for _ in range(3):
        thirds.append(lax.reduce_precision(rest, 8, 7))
        rest = rest - thirds[-1]
    thirds = jnp.stack(thirds, axis=1).reshape(dp_count, 3 * rows // wide, wide)
    used = 3 * units + thirds.shape[1]
    thirds = jnp.pad(thirds, ((0, 0), (0, round_up(used, 16) - used), (0, 0)))
    shared = deal(shared_gate, shared_up, shared_down, thirds)

    mine = [expert_gate[0].T, expert_up[0].T, expert_down[0]]
    other_attention = moves.swap_core(attention)
    residuals = moves.all_mp(residual)
    gains = moves.all_mp(ffn_gain.reshape(1, half))
    offsets, stacks, swapped = [], [], []

    def exchange(listed, own, beside):
        swapped.append(moves.swap_core(beside))
        for value, flip in ((own, False), (swapped[-1], True)):
            offsets.append([(offset, flip) for offset in listed])
            stacks.append(moves.all_mp(value))

    early = 1 + 2 * (left - 1)
    listed, filled = [0], 0
    sums = early
    arrived = [out_weight]
    ahead = behind = out_weight
    for s in range(1, left + 1):
        if s > 1:
            sums = project(attention, other_attention, arrived, filled, sums)
            filled += len(arrived)
            arrived = []
        if s == left:
            exchange(listed, *sums)
            listed = []
        moved = [moves.step(ahead, 1)]
        if s <= right:
            moved.append(moves.step(behind, -1))
        ties = []
        if s == left - 1:
            ties = [shared, *residuals[1:], *gains[1:]]
        if s > 1:
            ties += sums
        moved, ties = lax.optimization_barrier((moved, ties))
        if s > 1:
            sums = ties[-2:]
        if s == left - 1:
            shared = ties[0]
        ahead = moved[0]
        arrived.append(ahead)
        listed.append(-s)
        if s <= right:
            behind = moved[1]
            arrived.append(behind)
            listed.append(s)
    shared = lax.all_to_all(after(shared, ahead), "dp", 0, 0, tiled=True)
    other = [moves.swap_core(after(w, ahead)) for w in mine]
    exchange(listed, *project(attention, other_attention, arrived, 0, len(arrived)))
    normed, own_hidden = norm(
        info, offsets, [piece for stack in stacks for piece in stack], residuals, gains
    )
    shared = after(shared, normed).transpose(1, 0, 2)
    shared = [shared, moves.swap_core(shared)]

    def unpack(shared):
        spare = round_up(CORES * units, 16) - CORES * units
        parts = []
        for i in range(3):
            part = [value[i * units : (i + 1) * units].reshape(units, D) for value in shared]
            parts.append(jnp.pad(jnp.concatenate(part), ((0, spare), (0, 0))))
        weights = [*mine, *parts, *other]
        scores = []
        for value in shared:
            thirds = value[3 * units : used].transpose(1, 0, 2).reshape(dp_count, 3, rows)
            scores.append(jnp.sum(thirds.astype(f32), axis=1))
        return weights, scores

    def swap_mp(sent):
        return [moves.from_mp(sent[k - 1], mp_count - k) for k in range(1, mp_count)]

    gate = moves.from_mp(normed[:16, :LANES], 1)
    shared = [after(value, gate) for value in shared]
    weights, scores = unpack(shared)
    ahead = behind = normed
    done = []
    for s in range(1, left + 1):
        if s > 1:
            outs = list(ffn(listed, blocks, scores, weights, info, mp_count))
            done.append([listed, outs, None])
        if s <= right:
            moved = [moves.step(ahead, 1), moves.step(behind, -1)]
        else:
            moved = [moves.step(ahead, 1)]
        if s > 1:
            came = done[-2][2] if s > 2 else []
            moved, ties, came = lax.optimization_barrier((moved, outs[1:], came))
            if s > 2:
                done[-2][2] = came
            done[-1][2] = swap_mp(outs[1:])
        else:
            moved, weights[3:6], scores = lax.optimization_barrier((moved, weights[3:6], scores))
        ahead, behind, blocks = moved[0], moved[-1], moved
        listed = [-s, s] if s <= right else [s]
    outs = ffn([*listed, 0], [*blocks, normed], scores, weights, info, mp_count)
    for start, stop, offsets in (
        (0, rows * len(listed), listed),
        (rows * len(listed), rows * (len(listed) + 1), [0]),
    ):
        done.append([offsets, [value[start:stop] for value in outs], None])
    parts, whole = {}, {}
    for listed, (kept, *sent), came in done:
        if right in listed:
            for i, offset in enumerate(listed):
                whole[offset] = [value[i * rows : (i + 1) * rows] for value in (kept, *sent)]
            continue
        for value in swap_mp(sent) if came is None else came:
            kept = kept + value.astype(f32)
        for i, offset in enumerate(listed):
            parts[offset] = kept[i * rows : (i + 1) * rows]

    carried = []
    for way in (1, -1):
        kept, *sent = whole[way * right]
        came = [moves.step(kept.astype(bf16), way)]
        came += [moves.step_across(value, way, k + 1) for k, value in enumerate(sent)]
        for s in range(right - 1, 0, -1):
            part = parts[way * s]
            for value in came:
                part = part + value.astype(f32)
            came = [moves.step(part.astype(bf16), way)]
        carried += came
    mixture = parts[0]
    if left > right:
        carried.append(moves.step(parts[left].astype(bf16), left))
    for value in carried:
        mixture = mixture + value.astype(f32)

    final = (own_hidden.astype(f32) + mixture).astype(bf16)
    final_float = final.astype(f32)
    squares = moves.all_mp(jnp.sum(final_float * final_float, axis=1, keepdims=True).T)
    scale = lax.rsqrt(sum(squares) / D + EPSILON).T
    next_normed = (final_float * scale * next_gain).astype(bf16)
    return (final, next_normed)


def solution(mesh):
    in_specs = (
        P("dp", "mp"),
        P("dp", "mp"),
        P("mp", "dp"),
        P("mp"),
        P("dp", "mp"),
        P("dp", "mp"),
        P("mp", "dp"),
        P("dp", None, "mp"),
        P("dp", None, "mp"),
        P("dp", "mp", None),
        P("dp", None),
        P("dp", None),
        P(),
        P("mp"),
    )
    out_specs = (P("dp", "mp"), P("dp", "mp"))
    return jax.shard_map(local, mesh=mesh, in_specs=in_specs, out_specs=out_specs, check_vma=False)
```
